128 devices in a mesh: subj: 4 (over z_hi, core), depth: 32 (over y, z_lo, x).
Axes of the slice: x: 4, y: 4, z: 4 (z_hi: 2, z_lo: 2; z = z_hi * 2 + z_lo), core: 2. Of those that a mesh axis runs over, the one named last changes fastest.
Arguments:
- volumes: bfloat16 [4, 256, 256, 256], P('subj', 'depth'), may hold values from -6 to 6
- depth_shift: int32 [4, 32], P('subj', 'depth'), may hold values from -8 to 7
- plane_shift: int32 [4, 32, 2], P('subj', 'depth'), may hold values from -4 to 3
- fraction_steps: int32 [4, 32, 3], P('subj', 'depth'), may hold values from 0 to 3
Outputs:
- velocity: bfloat16 [4, 3, 256, 256, 256], P('subj', None, 'depth')
- template: bfloat16 [256, 256, 256], P('depth')
The draws below stay inside these ranges and needn't reach their ends.
All inputs are finite; a program needn't handle non-finite values.
Results may differ from the reference program's by a relative error of at most 0.018.
Values may be sent and summed in bfloat16 or wider, within the bound.
A program may use at most 128 MiB of HBM per device.

```python
import math
import jax
import jax.numpy as jnp
from jax import lax

H = 256
W = 256
BRICK = 8
MAXIN = 4
SUBJ = 4
DEPTH = 256
BRICKS = 32


def with_ends(values, stream_key, low, top_value):
    place = [jax.random.randint(jax.random.fold_in(stream_key, axis), (), 0, length) for axis, length in enumerate(values.shape)]
    widest = values.shape.index(max(values.shape))
    beside = place[:widest] + [(place[widest] + 1) % values.shape[widest]] + place[widest + 1:]
    return values.at[tuple(place)].set(low).at[tuple(beside)].set(top_value)


def block_scale(rng, dims, split, smallest, largest):
    loudness = 1.0
    for dim, parts in split:
        heights = jax.random.uniform(jax.random.fold_in(jax.random.fold_in(rng, 6), dim), (parts,), jnp.float32, smallest / len(split), largest / len(split))
        loudness = loudness * jnp.repeat(jnp.exp(heights), dims[dim] // parts).reshape((-1,) + (1,) * (len(dims) - 1 - dim))
    return loudness


def gaussian(stream_key, dims, scale, reach, shards=(), held_as=jnp.bfloat16):
    array = jax.random.normal(stream_key, dims, jnp.float32) * scale
    if len(shards) > 0:
        array = block_scale(stream_key, dims, shards, -0.22, 0.18) * array
    return jnp.clip(array, min=-reach, max=reach).astype(held_as)


def setup_inputs(seed: int = 0) -> dict:
    keys = jax.random.split(jax.random.key(seed), 5)
    return {
        "volumes": gaussian(keys[0], (SUBJ, DEPTH, H, W), 1.0, 6.0, ((0, 4), (1, 32))),
        "depth_shift": with_ends(jax.random.randint(keys[1], (SUBJ, BRICKS), 0 - BRICK, BRICK), jax.random.fold_in(keys[1], 1), 0 - BRICK, BRICK - 1).astype(jnp.int32),
        "plane_shift": with_ends(jax.random.randint(keys[2], (SUBJ, BRICKS, 2), 0 - MAXIN, MAXIN), jax.random.fold_in(keys[2], 1), 0 - MAXIN, MAXIN - 1).astype(jnp.int32),
        "fraction_steps": with_ends(jax.random.randint(keys[3], (SUBJ, BRICKS, 3), 0, 4), jax.random.fold_in(keys[3], 1), 0, 3).astype(jnp.int32),
    }


eps = 1e-5


def shift_lerp(field, offset, frac, axis):
    count = field.shape[axis]
    widths = [(0, 0)] * field.ndim
    widths[axis] = (MAXIN, MAXIN)
    padded = jnp.pad(field, widths)
    part = lax.dynamic_slice_in_dim(padded, offset + MAXIN, count + 1, axis)
    lower = lax.slice_in_dim(part, 0, count, axis=axis)
    upper = lax.slice_in_dim(part, 1, count + 1, axis=axis)
    return lower * (1.0 - frac) + upper * frac


def warp_subject(padded, shifts, planes, steps):
    bricks = shifts.shape[0]
    starts = jnp.arange(bricks, dtype=jnp.int32) * BRICK + BRICK + shifts.astype(jnp.int32)

    def one_brick(start, plane, step):
        rows = lax.dynamic_slice_in_dim(padded, start, BRICK + 1, 0).astype(jnp.float32)
        fracs = step.astype(jnp.float32) / 4.0
        inner = rows[:-1] * (1.0 - fracs[0]) + rows[1:] * fracs[0]
        inner = shift_lerp(inner, plane[0], fracs[1], 1)
        inner = shift_lerp(inner, plane[1], fracs[2], 2)
        return inner

    blocks = jax.vmap(one_brick)(starts, planes, steps)
    return blocks.reshape((bricks * BRICK,) + blocks.shape[2:]).astype(jnp.bfloat16)


def box_sum(field):
    count = field.shape[0] - 4
    height, width = field.shape[1], field.shape[2]
    total = field[0:count]
    for k in range(1, 5):
        total = total + field[k:k + count]
    padded = jnp.pad(total, ((0, 0), (2, 2), (0, 0)))
    total = padded[:, 0:height]
    for k in range(1, 5):
        total = total + padded[:, k:k + height]
    padded = jnp.pad(total, ((0, 0), (0, 0), (2, 2)))
    total = padded[:, :, 0:width]
    for k in range(1, 5):
        total = total + padded[:, :, k:k + width]
    return total


def force_of(image, templ):
    count = image.shape[0] - 4
    mean_i = box_sum(image) / 125.0
    mean_j = box_sum(templ) / 125.0
    cross = box_sum(image * templ) / 125.0 - mean_i * mean_j
    var_i = box_sum(image * image) / 125.0 - mean_i * mean_i + eps
    var_j = box_sum(templ * templ) / 125.0 - mean_j * mean_j + eps
    inner_i = image[2:2 + count]
    inner_j = templ[2:2 + count]
    factor = 2.0 * cross / (var_i * var_j)
    differ = (inner_j - mean_j) - (cross / var_i) * (inner_i - mean_i)
    grad_z = (image[3:3 + count] - image[1:1 + count]) * 0.5
    padded = jnp.pad(inner_i, ((0, 0), (1, 1), (0, 0)))
    grad_y = (padded[:, 2:] - padded[:, :-2]) * 0.5
    padded = jnp.pad(inner_i, ((0, 0), (0, 0), (1, 1)))
    grad_x = (padded[:, :, 2:] - padded[:, :, :-2]) * 0.5
    common = factor * differ
    return jnp.stack([common * grad_z, common * grad_y, common * grad_x])


def gauss_taps():
    raw = [math.exp(-(t * t) / 4.5) for t in range(-4, 5)]
    total = sum(raw)
    return [r / total for r in raw]


def smooth(field):
    taps = gauss_taps()
    count = field.shape[1] - 8
    height, width = field.shape[2], field.shape[3]
    total = taps[0] * field[:, 0:count]
    for k in range(1, 9):
        total = total + taps[k] * field[:, k:k + count]
    padded = jnp.pad(total, ((0, 0), (0, 0), (4, 4), (0, 0)))
    total = taps[0] * padded[:, :, 0:height]
    for k in range(1, 9):
        total = total + taps[k] * padded[:, :, k:k + height]
    padded = jnp.pad(total, ((0, 0), (0, 0), (0, 0), (4, 4)))
    total = taps[0] * padded[:, :, :, 0:width]
    for k in range(1, 9):
        total = total + taps[k] * padded[:, :, :, k:k + width]
    return total


def reference(volumes, depth_shift, plane_shift, fraction_steps):
    padded = jnp.pad(volumes, ((0, 0), (BRICK, BRICK), (0, 0), (0, 0)))
    warped = lax.map(lambda group: warp_subject(*group), (padded, depth_shift, plane_shift, fraction_steps))
    template = (jnp.sum(warped.astype(jnp.float32), 0) / SUBJ).astype(jnp.bfloat16)
    templ_ext = jnp.pad(template.astype(jnp.float32), ((2, 2), (0, 0), (0, 0)))

    def one_subject(image):
        image_ext = jnp.pad(image.astype(jnp.float32), ((2, 2), (0, 0), (0, 0)))
        force = force_of(image_ext, templ_ext).astype(jnp.bfloat16)
        force_ext = jnp.pad(force.astype(jnp.float32), ((0, 0), (4, 4), (0, 0), (0, 0)))
        return (8.0 * smooth(force_ext)).astype(jnp.bfloat16)

    velocity = lax.map(one_subject, warped)
    return velocity, template
```

```python
import math

import jax
import jax.numpy as jnp
from jax import lax
from jax.experimental import pallas as pl
from jax.experimental.pallas import tpu as pltpu
from jax.sharding import PartitionSpec as P

MESH = pl.DeviceIdType.MESH
F32, BF16 = jnp.float32, jnp.bfloat16
H = W = 256
B = 8
HALO = 6
NE = B + 2 * HALO
PAD = 16
EPS = 1e-5
SRC = (0, 64, 128, 192, 256)
C = len(SRC) - 1


def lagging(ends):
    return tuple(max(e - 16, 0) if e < H else H for e in ends)


WE = lagging(SRC)
FE = lagging(WE)
GE = lagging(FE)
NF = max(FE[i + 1] - FE[i] for i in range(C))
G = 16

SRC_R, SRC_L, W_R, W_L, W_C, S_Z, T_C, T_R, T_L, R_L, R_R = range(11)


def taps():
    raw = [math.exp(-(t * t) / 4.5) for t in range(-4, 5)]
    total = sum(raw)
    return [r / total for r in raw]


def iota(shape, dim):
    return lax.broadcasted_iota(jnp.int32, shape, dim)


def gauss_matrix(rows, cols, shift):
    away = jnp.abs(iota((rows, cols), 0) + shift - iota((rows, cols), 1))
    w = taps()
    out = jnp.zeros((rows, cols), F32)
    for t in range(5):
        out = jnp.where(away == t, F32(w[4 + t]), out)
    return out.astype(BF16)


def dot(a, b):
    return jnp.dot(a, b, preferred_element_type=F32)


def rounded_gain():
    import numpy as np
    import ml_dtypes
    w = np.array(taps(), np.float32)
    return float(w.sum()) / float(w.astype(ml_dtypes.bfloat16).astype(np.float32).sum())


def kernel(vol, dsh, psh, fst, vel, tmpl, *refs):
    ext = refs[:C]
    (iext, text, wp, sb, sz, yb, gy, sp, bq, fo, zs, vst, ax2, bx3, dx, gx, ssem, rsem, lsem) = refs[C:]
    me, d = lax.axis_index("subj"), lax.axis_index("depth")
    nd = lax.axis_size("depth")
    core = lax.rem(me, 2)
    mate = me + 1 - 2 * core
    far = lax.rem(me + 2, 4)
    right, left = lax.rem(d + 1, nd), lax.rem(d + nd - 1, nd)
    has_l, has_r = d > 0, d < nd - 1

    def remote(src, dst, p, kind, subj, depth):
        return pltpu.make_async_remote_copy(
            src_ref=src, dst_ref=dst, send_sem=ssem.at[p, kind], recv_sem=rsem.at[p, kind],
            device_id={"subj": subj, "depth": depth}, device_id_type=MESH)

    barrier = pltpu.get_barrier_semaphore()

    def greet(subj, depth):
        pl.semaphore_signal(barrier, inc=1, device_id={"subj": subj, "depth": depth}, device_id_type=MESH)

    greet(mate, d)
    greet(far, d)

    @pl.when(has_l)
    def _():
        greet(me, left)

    @pl.when(has_r)
    def _():
        greet(me, right)

    mine = pl.ds(pl.multiple_of(core * 128, 128), 128)
    other = pl.ds(pl.multiple_of((1 - core) * 128, 128), 128)

    def rows_of(ends, p):
        return pl.ds(ends[p], ends[p + 1] - ends[p])

    def padded_rows(ends, p):
        return pl.ds(PAD + ends[p], ends[p + 1] - ends[p])

    def copy_of(p, kind):
        if kind == SRC_R:
            return remote(vol.at[:, rows_of(SRC, p), :], ext[p].at[0:B], p, kind, me, right)
        if kind == SRC_L:
            return remote(vol.at[:, rows_of(SRC, p), :], ext[p].at[2 * B:3 * B], p, kind, me, left)
        r, q = rows_of(WE, p), padded_rows(WE, p)
        if kind == W_R:
            return remote(iext.at[B:B + HALO, q, :], iext.at[0:HALO, q, :], p, kind, me, right)
        if kind == W_L:
            return remote(iext.at[HALO:2 * HALO, q, :], iext.at[B + HALO:NE, q, :], p, kind, me, left)
        if kind == W_C:
            return remote(iext.at[HALO:HALO + B, q, other], wp.at[:, r, :], p, kind, mate, d)
        if kind == S_Z:
            return remote(sb.at[:, r, :], sz.at[:, r, :], p, kind, far, d)
        if kind == T_C:
            part = text.at[HALO:HALO + B, q, mine]
            return remote(part, part, p, kind, mate, d)
        if kind == T_R:
            return remote(text.at[B:B + HALO, q, mine], text.at[0:HALO, q, mine], p, kind, me, right)
        if kind == T_L:
            return remote(text.at[HALO:2 * HALO, q, mine], text.at[B + HALO:NE, q, mine], p, kind, me, left)
        part = text.at[0:HALO, q, mine] if kind == R_L else text.at[B + HALO:NE, q, mine]
        return remote(part, part, p, kind, mate, d)

    sends = {SRC_R: has_r, W_R: has_r, T_R: has_r, SRC_L: has_l, W_L: has_l, T_L: has_l, R_L: has_l, R_R: has_r}
    gets = {SRC_R: has_l, W_R: has_l, T_R: has_l, SRC_L: has_r, W_L: has_r, T_L: has_r, R_L: has_l, R_R: has_r}

    def start(p, *kinds):
        for kind in kinds:
            if kind in sends:
                pl.when(sends[kind])(lambda kind=kind: copy_of(p, kind).start())
            else:
                copy_of(p, kind).start()

    def landed(p, *kinds):
        for kind in kinds:
            if kind in gets:
                pl.when(gets[kind])(lambda kind=kind: copy_of(p, kind).wait_recv())
            else:
                copy_of(p, kind).wait_recv()

    def own_copy(p):
        return pltpu.make_async_copy(vol.at[:, rows_of(SRC, p), :], ext[p].at[B:2 * B], lsem.at[p])

    for p in range(C):
        own_copy(p).start()

    pl.semaphore_wait(barrier, 2 + has_l.astype(jnp.int32) + has_r.astype(jnp.int32))
    for p in range(C):
        start(p, SRC_R, SRC_L)

    dz, dy, dxs = dsh[0], psh[0], psh[1]
    fz, fy, fx = fst[0].astype(F32) * 0.25, fst[1].astype(F32) * 0.25, fst[2].astype(F32) * 0.25

    def zero_pads(ref, count):
        zero = jnp.zeros((PAD, W), BF16)

        def body(z, carry):
            ref[z, 0:PAD, :] = zero
            ref[z, PAD + H:2 * PAD + H, :] = zero
            return carry
        lax.fori_loop(0, count, body, 0)

    zero_pads(iext, NE)
    zero_pads(text, NE)
    for k in range(3):
        zero_pads(zs.at[k], B)

    def zero_planes(lo):
        def body(z, carry):
            zero = jnp.zeros((H, W), BF16)
            iext[lo + z, PAD:PAD + H, :] = zero
            text[lo + z, PAD:PAD + H, :] = zero
            return carry
        lax.fori_loop(0, HALO, body, 0)

    @pl.when(d == 0)
    def _():
        zero_planes(0)
        for p in range(C):
            ext[p][0:B] = jnp.zeros((B,) + ext[p].shape[1:], BF16)

    @pl.when(d == nd - 1)
    def _():
        zero_planes(B + HALO)
        for p in range(C):
            ext[p][2 * B:3 * B] = jnp.zeros((B,) + ext[p].shape[1:], BF16)

    row, col = iota((W, W), 0), iota((W, W), 1)
    a_x = jnp.where(row == col + dxs, 1.0 - fx, jnp.where(row == col + dxs + 1, fx, 0.0)).astype(BF16)
    ax2[0:W, :] = a_x
    ax2[W:2 * W, :] = a_x
    b_x = jnp.where(jnp.abs(row - col) <= 2, 1.0, 0.0).astype(BF16)
    for i in range(3):
        bx3[i * W:(i + 1) * W, :] = b_x
    dx[...] = jnp.where(row == col + 1, 0.5, jnp.where(row == col - 1, -0.5, 0.0)).astype(BF16)
    gx[...] = gauss_matrix(W, W, 0)

    def warp(p):
        a, n = WE[p], WE[p + 1] - WE[p]
        ka = 0 if p == 0 else SRC[p] - 32
        k = SRC[p + 1] - ka
        at, j = iota((n, 2 * k), 0) + (a + dy), iota((n, 2 * k), 1)
        w_z = jnp.where(j < k, 1.0 - fz, fz)
        j = jnp.where(j < k, j, j - k) + ka
        a_y = (w_z * jnp.where(j == at, 1.0 - fy, jnp.where(j == at + 1, fy, 0.0))).astype(BF16)

        def body(z, carry):
            parts = []
            for c in range(2):
                if p > 0:
                    size = SRC[p] - SRC[p - 1]
                    parts.append(ext[p - 1][8 + dz + z + c, size - 32:size, :])
                parts.append(ext[p][8 + dz + z + c])
            r = dot(a_y, jnp.concatenate(parts, 0))
            hi = r.astype(BF16)
            lo = (r - hi.astype(F32)).astype(BF16)
            out = dot(jnp.concatenate([hi, lo], 1), ax2[...])
            iext[HALO + z, PAD + a:PAD + a + n, :] = out.astype(BF16)
            return carry
        lax.fori_loop(0, B, body, 0)

    def partial_sum(p):
        r, q = rows_of(WE, p), padded_rows(WE, p)

        def body(z, carry):
            sb[z, r, :] = (iext[HALO + z, q, mine].astype(F32) + wp[z, r, :].astype(F32)).astype(BF16)
            return carry
        lax.fori_loop(0, B, body, 0)

    def template(p):
        r, q = rows_of(WE, p), padded_rows(WE, p)

        def body(z, carry):
            text[HALO + z, q, mine] = ((sb[z, r, :].astype(F32) + sz[z, r, :].astype(F32)) * 0.25).astype(BF16)
            return carry
        lax.fori_loop(0, B, body, 0)

    def force(p):
        a, n = FE[p], FE[p + 1] - FE[p]
        k = n + 2 * PAD
        away = iota((n, k), 0) + PAD - iota((n, k), 1)
        b_y = jnp.where(jnp.abs(away) <= 2, 1.0, 0.0).astype(BF16)
        d_y = jnp.where(away == -1, 0.5, jnp.where(away == 1, -0.5, 0.0)).astype(BF16)
        bd = jnp.concatenate([b_y, d_y], 0)
        b2 = jnp.concatenate([b_y, b_y], 1)

        def in_rows(z, carry):
            i, j = iext[z, a:a + k, :], text[z, a:a + k, :]
            both = dot(bd, i)
            yb[0, z, 0:n, :] = both[:n]
            gy[z, 0:n, :] = both[n:]
            yb[1, z, 0:n, :] = dot(b_y, j)
            fi, fj = i.astype(F32), j.astype(F32)
            for q, v in ((2, fi * fj), (3, fi * fi), (4, fj * fj)):
                hi = v.astype(BF16)
                lo = (v - hi.astype(F32)).astype(BF16)
                yb[q, z, 0:n, :] = dot(b2, jnp.concatenate([hi, lo], 0))
            return carry
        lax.fori_loop(0, NE, in_rows, 0)

        def plane(z, carry):
            for g in range(0, n, G):
                for q in range(5):
                    s = yb[q, z, g:g + G, :]
                    for t in range(1, 5):
                        s = s + yb[q, z + t, g:g + G, :]
                    for part in range(3):
                        piece = s.astype(BF16)
                        sp[q * n + g:q * n + g + G, part * W:(part + 1) * W] = piece
                        s = s - piece.astype(F32)
            bq[0:5 * n, :] = dot(sp[0:5 * n, :], bx3[...])
            whole = (d * B - 4 + z >= 0) & (d * B - 4 + z < nd * B)
            g_x = dot(iext[z + 2, PAD + a:PAD + a + n, :], dx[...])
            for g in range(0, n, G):
                here = slice(PAD + a + g, PAD + a + g + G)
                m_i, m_j = bq[g:g + G, :] * (1 / 125), bq[n + g:n + g + G, :] * (1 / 125)
                cov = bq[2 * n + g:2 * n + g + G, :] * (1 / 125) - m_i * m_j
                v_i = bq[3 * n + g:3 * n + g + G, :] * (1 / 125) - m_i * m_i + EPS
                v_j = bq[4 * n + g:4 * n + g + G, :] * (1 / 125) - m_j * m_j + EPS
                scaled = cov / (v_i * v_j)
                i, j = iext[z + 2, here, :].astype(F32), text[z + 2, here, :].astype(F32)
                common = 2.0 * scaled * ((j - m_j) - scaled * v_j * (i - m_i))
                common = jnp.where(whole, common, 0.0)
                g_z = (iext[z + 3, here, :].astype(F32) - iext[z + 1, here, :].astype(F32)) * 0.5
                fo[0, z, g:g + G, :] = (common * g_z).astype(BF16)
                fo[1, z, g:g + G, :] = (common * gy[z + 2, g:g + G, :]).astype(BF16)
                fo[2, z, g:g + G, :] = (common * g_x[g:g + G]).astype(BF16)
            return carry
        lax.fori_loop(0, 2 * B, plane, 0)

        w = [8.0 * rounded_gain() ** 2 * t for t in taps()]

        def along_depth(g, carry):
            r = pl.ds(pl.multiple_of(g * G, G), G)
            out = pl.ds(pl.multiple_of(PAD + a + g * G, G), G)
            for k3 in range(3):
                for half in range(2):
                    lanes = slice(half * 128, half * 128 + 128)
                    f = [fo[k3, z, r, lanes].astype(F32) for z in range(2 * B)]
                    for z in range(B):
                        s = f[z + 4] * w[4]
                        for t in range(1, 5):
                            s = s + (f[z + 4 - t] + f[z + 4 + t]) * w[4 + t]
                        zs[k3, z, out, lanes] = s.astype(BF16)
            return carry
        lax.fori_loop(0, n // G, along_depth, 0)

    def out_copy(p):
        r = rows_of(GE, p)
        return pltpu.make_async_copy(vst.at[:, :, r, :], vel.at[:, :, r, :], lsem.at[C + p])

    def smooth(p):
        a, n = GE[p], GE[p + 1] - GE[p]
        if n == 0:
            return
        g_y = gauss_matrix(n, n + 2 * PAD, PAD)

        def body(z, carry):
            for k3 in range(3):
                r = dot(g_y, zs[k3, z, a:a + n + 2 * PAD, :]).astype(BF16)
                vst[k3, z, a:a + n, :] = dot(r, gx[...]).astype(BF16)
            return carry
        lax.fori_loop(0, B, body, 0)
        out_copy(p).start()

    for t in range(C + 3):
        if t < C:
            own_copy(t).wait()
            landed(t, SRC_R, SRC_L)
            warp(t)
            start(t, W_C, W_R, W_L)
            landed(t, W_C)
            partial_sum(t)
            start(t, S_Z)
        p = t - 1
        if 0 <= p < C:
            landed(p, S_Z)
            template(p)
            start(p, T_R, T_L, T_C)
        p = t - 2
        if 0 <= p < C:
            landed(p, T_R, T_L)
            start(p, R_L, R_R)
        p = t - 3
        if 0 <= p < C:
            landed(p, W_R, W_L, T_C, R_L, R_R)
            if p == C - 1:
                whole_template = pltpu.make_async_copy(
                    text.at[HALO:HALO + B, PAD:PAD + H, :], tmpl, lsem.at[2 * C])
                whole_template.start()
            force(p)
            smooth(p)

    for p in range(C):
        if GE[p + 1] > GE[p]:
            out_copy(p).wait()
    whole_template.wait()
    for p in range(C):
        for kind in range(11):
            if kind in sends:
                pl.when(sends[kind])(lambda kind=kind: copy_of(p, kind).wait_send())
            else:
                copy_of(p, kind).wait_send()


def shards(volumes, depth_shift, plane_shift, fraction_steps):
    smem = pl.BlockSpec(memory_space=pltpu.SMEM)
    anywhere = pl.BlockSpec(memory_space=pl.ANY)
    scratch = [pltpu.VMEM((3 * B, SRC[p + 1] - SRC[p], W), BF16) for p in range(C)]
    scratch += [
        pltpu.VMEM((NE, H + 2 * PAD, W), BF16),
        pltpu.VMEM((NE, H + 2 * PAD, W), BF16),
        pltpu.VMEM((B, H, 128), BF16),
        pltpu.VMEM((B, H, 128), BF16),
        pltpu.VMEM((B, H, 128), BF16),
        pltpu.VMEM((5, NE, NF, W), F32),
        pltpu.VMEM((NE, NF, W), F32),
        pltpu.VMEM((5 * NF, 3 * W), BF16),
        pltpu.VMEM((5 * NF, W), F32),
        pltpu.VMEM((3, 2 * B, NF, W), BF16),
        pltpu.VMEM((3, B, H + 2 * PAD, W), BF16),
        pltpu.VMEM((3, B, H, W), BF16),
        pltpu.VMEM((2 * W, W), BF16),
        pltpu.VMEM((3 * W, W), BF16),
        pltpu.VMEM((W, W), BF16),
        pltpu.VMEM((W, W), BF16),
        pltpu.SemaphoreType.DMA((C, 11)),
        pltpu.SemaphoreType.DMA((C, 11)),
        pltpu.SemaphoreType.DMA((2 * C + 1,)),
    ]
    velocity, template = pl.pallas_call(
        kernel,
        out_shape=(jax.ShapeDtypeStruct((3, B, H, W), BF16), jax.ShapeDtypeStruct((B, H, W), BF16)),
        in_specs=[anywhere, smem, smem, smem],
        out_specs=(anywhere, anywhere),
        scratch_shapes=scratch,
        compiler_params=pltpu.CompilerParams(
            collective_id=0, has_side_effects=True, vmem_limit_bytes=56 * 1024 * 1024),
    )(volumes[0], depth_shift.reshape(1), plane_shift.reshape(2), fraction_steps.reshape(3))
    return velocity[None], template


def solution(mesh):
    return jax.shard_map(
        shards,
        mesh=mesh,
        in_specs=(
            P("subj", "depth", None, None),
            P("subj", "depth"),
            P("subj", "depth", None),
            P("subj", "depth", None),
        ),
        out_specs=(P("subj", None, "depth", None, None), P("depth", None, None)),
        check_vma=False,
    )
```

```python
import math

import jax
import jax.numpy as jnp
from jax import lax
from jax.experimental import pallas as pl
from jax.experimental.pallas import tpu as pltpu
from jax.sharding import PartitionSpec as P

MESH = pl.DeviceIdType.MESH
F32, BF16 = jnp.float32, jnp.bfloat16
H = W = 256
B = 8
HALO = 6
NE = B + 2 * HALO
PAD = 16
EPS = 1e-5
SRC = (0, 64, 128, 192, 256)
C = len(SRC) - 1


def lagging(ends):
    return tuple(max(e - 16, 0) if e < H else H for e in ends)


WE = lagging(SRC)
FE = lagging(WE)
GE = lagging(FE)
NF = max(FE[i + 1] - FE[i] for i in range(C))
G = 16
U = 4

SRC_R, SRC_L, W_R, W_L, W_C, S_Z, T_C, T_R, T_L, R_L, R_R = range(11)


def taps():
    raw = [math.exp(-(t * t) / 4.5) for t in range(-4, 5)]
    total = sum(raw)
    return [r / total for r in raw]


def iota(shape, dim):
    return lax.broadcasted_iota(jnp.int32, shape, dim)


def gauss_matrix(rows, cols, shift):
    away = jnp.abs(iota((rows, cols), 0) + shift - iota((rows, cols), 1))
    w = taps()
    out = jnp.zeros((rows, cols), F32)
    for t in range(5):
        out = jnp.where(away == t, F32(w[4 + t]), out)
    return out.astype(BF16)


def dot(a, b):
    return jnp.dot(a, b, preferred_element_type=F32)


def rounded_gain():
    import numpy as np
    import ml_dtypes
    w = np.array(taps(), np.float32)
    return float(w.sum()) / float(w.astype(ml_dtypes.bfloat16).astype(np.float32).sum())


def kernel(vol, dsh, psh, fst, vel, tmpl, *refs):
    ext = refs[:C]
    (iext, text, wp, sb, sz, yb, gy, sp, bq, gxs, fo, zs, vst, ax2, bx3, dx, gx, ssem, rsem, lsem) = refs[C:]
    me, d = lax.axis_index("subj"), lax.axis_index("depth")
    nd = lax.axis_size("depth")
    core = lax.rem(me, 2)
    mate = me + 1 - 2 * core
    far = lax.rem(me + 2, 4)
    right, left = lax.rem(d + 1, nd), lax.rem(d + nd - 1, nd)
    has_l, has_r = d > 0, d < nd - 1

    def remote(src, dst, p, kind, subj, depth):
        return pltpu.make_async_remote_copy(
            src_ref=src, dst_ref=dst, send_sem=ssem.at[p, kind], recv_sem=rsem.at[p, kind],
            device_id={"subj": subj, "depth": depth}, device_id_type=MESH)

    barrier = pltpu.get_barrier_semaphore()

    def greet(subj, depth):
        pl.semaphore_signal(barrier, inc=1, device_id={"subj": subj, "depth": depth}, device_id_type=MESH)

    greet(mate, d)
    greet(far, d)

    @pl.when(has_l)
    def _():
        greet(me, left)

    @pl.when(has_r)
    def _():
        greet(me, right)

    mine = pl.ds(pl.multiple_of(core * 128, 128), 128)
    other = pl.ds(pl.multiple_of((1 - core) * 128, 128), 128)

    def rows_of(ends, p):
        return pl.ds(ends[p], ends[p + 1] - ends[p])

    def padded_rows(ends, p):
        return pl.ds(PAD + ends[p], ends[p + 1] - ends[p])

    def copy_of(p, kind):
        if kind == SRC_R:
            return remote(vol.at[:, rows_of(SRC, p), :], ext[p].at[0:B], p, kind, me, right)
        if kind == SRC_L:
            return remote(vol.at[:, rows_of(SRC, p), :], ext[p].at[2 * B:3 * B], p, kind, me, left)
        r, q = rows_of(WE, p), padded_rows(WE, p)
        if kind == W_R:
            return remote(iext.at[B:B + HALO, q, :], iext.at[0:HALO, q, :], p, kind, me, right)
        if kind == W_L:
            return remote(iext.at[HALO:2 * HALO, q, :], iext.at[B + HALO:NE, q, :], p, kind, me, left)
        if kind == W_C:
            return remote(iext.at[HALO:HALO + B, q, other], wp.at[:, r, :], p, kind, mate, d)
        if kind == S_Z:
            return remote(sb.at[:, r, :], sz.at[:, r, :], p, kind, far, d)
        if kind == T_C:
            part = text.at[HALO:HALO + B, q, mine]
            return remote(part, part, p, kind, mate, d)
        if kind == T_R:
            return remote(text.at[B:B + HALO, q, mine], text.at[0:HALO, q, mine], p, kind, me, right)
        if kind == T_L:
            return remote(text.at[HALO:2 * HALO, q, mine], text.at[B + HALO:NE, q, mine], p, kind, me, left)
        part = text.at[0:HALO, q, mine] if kind == R_L else text.at[B + HALO:NE, q, mine]
        return remote(part, part, p, kind, mate, d)

    sends = {SRC_R: has_r, W_R: has_r, T_R: has_r, SRC_L: has_l, W_L: has_l, T_L: has_l, R_L: has_l, R_R: has_r}
    gets = {SRC_R: has_l, W_R: has_l, T_R: has_l, SRC_L: has_r, W_L: has_r, T_L: has_r, R_L: has_l, R_R: has_r}

    def start(p, *kinds):
        for kind in kinds:
            if kind in sends:
                pl.when(sends[kind])(lambda kind=kind: copy_of(p, kind).start())
            else:
                copy_of(p, kind).start()

    def landed(p, *kinds):
        for kind in kinds:
            if kind in gets:
                pl.when(gets[kind])(lambda kind=kind: copy_of(p, kind).wait_recv())
            else:
                copy_of(p, kind).wait_recv()

    def own_copy(p):
        return pltpu.make_async_copy(vol.at[:, rows_of(SRC, p), :], ext[p].at[B:2 * B], lsem.at[p])

    for p in range(C):
        own_copy(p).start()

    pl.semaphore_wait(barrier, 2 + has_l.astype(jnp.int32) + has_r.astype(jnp.int32))
    for p in range(C):
        start(p, SRC_R, SRC_L)

    dz, dy, dxs = dsh[0], psh[0], psh[1]
    fz, fy, fx = fst[0].astype(F32) * 0.25, fst[1].astype(F32) * 0.25, fst[2].astype(F32) * 0.25

    def zero_pads(ref, count):
        zero = jnp.zeros((PAD, W), BF16)

        def body(z, carry):
            ref[z, 0:PAD, :] = zero
            ref[z, PAD + H:2 * PAD + H, :] = zero
            return carry
        lax.fori_loop(0, count, body, 0)

    zero_pads(iext, NE)
    zero_pads(text, NE)
    for k in range(3):
        zero_pads(zs.at[k], B)

    def zero_planes(lo):
        def body(z, carry):
            zero = jnp.zeros((H, W), BF16)
            iext[lo + z, PAD:PAD + H, :] = zero
            text[lo + z, PAD:PAD + H, :] = zero
            return carry
        lax.fori_loop(0, HALO, body, 0)

    @pl.when(d == 0)
    def _():
        zero_planes(0)
        for p in range(C):
            ext[p][0:B] = jnp.zeros((B,) + ext[p].shape[1:], BF16)

    @pl.when(d == nd - 1)
    def _():
        zero_planes(B + HALO)
        for p in range(C):
            ext[p][2 * B:3 * B] = jnp.zeros((B,) + ext[p].shape[1:], BF16)

    row, col = iota((W, W), 0), iota((W, W), 1)
    a_x = jnp.where(row == col + dxs, 1.0 - fx, jnp.where(row == col + dxs + 1, fx, 0.0)).astype(BF16)
    ax2[0:W, :] = a_x
    ax2[W:2 * W, :] = a_x
    b_x = jnp.where(jnp.abs(row - col) <= 2, 1.0, 0.0).astype(BF16)
    for i in range(3):
        bx3[i * W:(i + 1) * W, :] = b_x
    dx[...] = jnp.where(row == col + 1, 0.5, jnp.where(row == col - 1, -0.5, 0.0)).astype(BF16)
    gx[...] = gauss_matrix(W, W, 0)

    def warp(p):
        a, n = WE[p], WE[p + 1] - WE[p]
        ka = 0 if p == 0 else SRC[p] - 32
        k = SRC[p + 1] - ka
        at, j = iota((n, 2 * k), 0) + (a + dy), iota((n, 2 * k), 1)
        w_z = jnp.where(j < k, 1.0 - fz, fz)
        j = jnp.where(j < k, j, j - k) + ka
        a_y = (w_z * jnp.where(j == at, 1.0 - fy, jnp.where(j == at + 1, fy, 0.0))).astype(BF16)

        for half in range(0, B, U):
            split = []
            for z in range(half, half + U):
                parts = []
                for c in range(2):
                    if p > 0:
                        size = SRC[p] - SRC[p - 1]
                        parts.append(ext[p - 1][8 + dz + z + c, size - 32:size, :])
                    parts.append(ext[p][8 + dz + z + c])
                r = dot(a_y, jnp.concatenate(parts, 0))
                hi = r.astype(BF16)
                lo = (r - hi.astype(F32)).astype(BF16)
                split.append(jnp.concatenate([hi, lo], 1))
            out = dot(jnp.concatenate(split, 0), ax2[...]).astype(BF16)
            iext[HALO + half:HALO + half + U, PAD + a:PAD + a + n, :] = out.reshape(U, n, W)

    def partial_sum(p):
        r, q = rows_of(WE, p), padded_rows(WE, p)

        def body(z, carry):
            sb[z, r, :] = (iext[HALO + z, q, mine].astype(F32) + wp[z, r, :].astype(F32)).astype(BF16)
            return carry
        lax.fori_loop(0, B, body, 0)

    def template(p):
        r, q = rows_of(WE, p), padded_rows(WE, p)

        def body(z, carry):
            text[HALO + z, q, mine] = ((sb[z, r, :].astype(F32) + sz[z, r, :].astype(F32)) * 0.25).astype(BF16)
            return carry
        lax.fori_loop(0, B, body, 0)

    def force(p):
        a, n = FE[p], FE[p + 1] - FE[p]
        k = n + 2 * PAD
        away = iota((n, k), 0) + PAD - iota((n, k), 1)
        b_y = jnp.where(jnp.abs(away) <= 2, 1.0, 0.0).astype(BF16)
        d_y = jnp.where(away == -1, 0.5, jnp.where(away == 1, -0.5, 0.0)).astype(BF16)
        bd = jnp.concatenate([b_y, d_y], 0)
        b2 = jnp.concatenate([b_y, b_y], 1)

        def in_rows(z):
            i, j = iext[z, a:a + k, :], text[z, a:a + k, :]
            both = dot(bd, i)
            yb[0, z, 0:n, :] = both[:n]
            gy[z, 0:n, :] = both[n:]
            yb[1, z, 0:n, :] = dot(b_y, j)
            fi, fj = i.astype(F32), j.astype(F32)
            for q, v in ((2, fi * fj), (3, fi * fi), (4, fj * fj)):
                hi = v.astype(BF16)
                lo = (v - hi.astype(F32)).astype(BF16)
                yb[q, z, 0:n, :] = dot(b2, jnp.concatenate([hi, lo], 0))

        def in_rows_of(zu, carry):
            for u in range(U):
                in_rows(zu * U + u)
            return carry
        lax.fori_loop(0, NE // U, in_rows_of, 0)

        def planes(zu, carry):
            z0 = zu * U
            for q in range(5):
                for g in range(0, n, G):
                    v = [yb[q, z0 + t, g:g + G, :] for t in range(8)]
                    m12, m34, m56 = v[1] + v[2], v[3] + v[4], v[5] + v[6]
                    low, high = m12 + m34, m34 + m56
                    for u, s in enumerate((v[0] + low, low + v[5], v[2] + high, high + v[7])):
                        at = (u * 5 + q) * n + g
                        for part in range(3):
                            piece = s.astype(BF16)
                            sp[at:at + G, part * W:(part + 1) * W] = piece
                            if part < 2:
                                s = s - piece.astype(F32)
            bq[0:5 * U * n, :] = dot(sp[0:5 * U * n, :], bx3[...])
            gxs[0:U * n, :] = dot(iext[pl.ds(z0 + 2, U), PAD + a:PAD + a + n, :].reshape(U * n, W), dx[...])
            for u in range(U):
                z = z0 + u
                whole = (d * B - 4 + z >= 0) & (d * B - 4 + z < nd * B)
                for g in range(0, n, G):
                    here = slice(PAD + a + g, PAD + a + g + G)
                    b_i, b_j, b_ij, b_ii, b_jj = (
                        bq[(u * 5 + q) * n + g:(u * 5 + q) * n + g + G, :] * (1 / 125) for q in range(5))
                    cov = b_ij - b_i * b_j
                    v_i = b_ii - b_i * b_i + EPS
                    v_j = b_jj - b_j * b_j + EPS
                    scaled = cov / (v_i * v_j)
                    i, j = iext[z + 2, here, :].astype(F32), text[z + 2, here, :].astype(F32)
                    common = 2.0 * scaled * ((j - b_j) - scaled * v_j * (i - b_i))
                    common = jnp.where(whole, common, 0.0)
                    g_z = (iext[z + 3, here, :].astype(F32) - iext[z + 1, here, :].astype(F32)) * 0.5
                    fo[0, z, g:g + G, :] = (common * g_z).astype(BF16)
                    fo[1, z, g:g + G, :] = (common * gy[z + 2, g:g + G, :]).astype(BF16)
                    fo[2, z, g:g + G, :] = (common * gxs[u * n + g:u * n + g + G, :]).astype(BF16)
            return carry
        lax.fori_loop(0, 2 * B // U, planes, 0)

        w = [8.0 * rounded_gain() ** 2 * t for t in taps()]

        def along_depth(g, carry):
            r = pl.ds(pl.multiple_of(g * G, G), G)
            out = pl.ds(pl.multiple_of(PAD + a + g * G, G), G)
            for k3 in range(3):
                for half in range(2):
                    lanes = slice(half * 128, half * 128 + 128)
                    f = [fo[k3, z, r, lanes].astype(F32) for z in range(2 * B)]
                    for z in range(B):
                        s = f[z + 4] * w[4]
                        for t in range(1, 5):
                            s = s + (f[z + 4 - t] + f[z + 4 + t]) * w[4 + t]
                        zs[k3, z, out, lanes] = s.astype(BF16)
            return carry
        lax.fori_loop(0, n // G, along_depth, 0)

    def out_copy(p):
        r = rows_of(GE, p)
        return pltpu.make_async_copy(vst.at[:, :, r, :], vel.at[:, :, r, :], lsem.at[C + p])

    def smooth(p):
        a, n = GE[p], GE[p + 1] - GE[p]
        if n == 0:
            return
        g_y = gauss_matrix(n, n + 2 * PAD, PAD)

        for k3 in range(3):
            for z in range(0, B, U):
                r = [dot(g_y, zs[k3, z + u, a:a + n + 2 * PAD, :]).astype(BF16) for u in range(U)]
                out = dot(jnp.concatenate(r, 0), gx[...]).astype(BF16)
                vst[k3, z:z + U, a:a + n, :] = out.reshape(U, n, W)
        out_copy(p).start()

    for t in range(C + 3):
        if t < C:
            own_copy(t).wait()
            landed(t, SRC_R, SRC_L)
            warp(t)
            start(t, W_C, W_R, W_L)
            landed(t, W_C)
            partial_sum(t)
            start(t, S_Z)
        p = t - 1
        if 0 <= p < C:
            landed(p, S_Z)
            template(p)
            start(p, T_R, T_L, T_C)
        p = t - 2
        if 0 <= p < C:
            landed(p, T_R, T_L)
            start(p, R_L, R_R)
        p = t - 3
        if 0 <= p < C:
            landed(p, W_R, W_L, T_C, R_L, R_R)
            if p == C - 1:
                whole_template = pltpu.make_async_copy(
                    text.at[HALO:HALO + B, PAD:PAD + H, :], tmpl, lsem.at[2 * C])
                whole_template.start()
            force(p)
            smooth(p)

    for p in range(C):
        if GE[p + 1] > GE[p]:
            out_copy(p).wait()
    whole_template.wait()
    for p in range(C):
        for kind in range(11):
            if kind in sends:
                pl.when(sends[kind])(lambda kind=kind: copy_of(p, kind).wait_send())
            else:
                copy_of(p, kind).wait_send()


def shards(volumes, depth_shift, plane_shift, fraction_steps):
    smem = pl.BlockSpec(memory_space=pltpu.SMEM)
    anywhere = pl.BlockSpec(memory_space=pl.ANY)
    scratch = [pltpu.VMEM((3 * B, SRC[p + 1] - SRC[p], W), BF16) for p in range(C)]
    scratch += [
        pltpu.VMEM((NE, H + 2 * PAD, W), BF16),
        pltpu.VMEM((NE, H + 2 * PAD, W), BF16),
        pltpu.VMEM((B, H, 128), BF16),
        pltpu.VMEM((B, H, 128), BF16),
        pltpu.VMEM((B, H, 128), BF16),
        pltpu.VMEM((5, NE, NF, W), F32),
        pltpu.VMEM((NE, NF, W), F32),
        pltpu.VMEM((5 * U * NF, 3 * W), BF16),
        pltpu.VMEM((5 * U * NF, W), F32),
        pltpu.VMEM((U * NF, W), F32),
        pltpu.VMEM((3, 2 * B, NF, W), BF16),
        pltpu.VMEM((3, B, H + 2 * PAD, W), BF16),
        pltpu.VMEM((3, B, H, W), BF16),
        pltpu.VMEM((2 * W, W), BF16),
        pltpu.VMEM((3 * W, W), BF16),
        pltpu.VMEM((W, W), BF16),
        pltpu.VMEM((W, W), BF16),
        pltpu.SemaphoreType.DMA((C, 11)),
        pltpu.SemaphoreType.DMA((C, 11)),
        pltpu.SemaphoreType.DMA((2 * C + 1,)),
    ]
    velocity, template = pl.pallas_call(
        kernel,
        out_shape=(jax.ShapeDtypeStruct((3, B, H, W), BF16), jax.ShapeDtypeStruct((B, H, W), BF16)),
        in_specs=[anywhere, smem, smem, smem],
        out_specs=(anywhere, anywhere),
        scratch_shapes=scratch,
        compiler_params=pltpu.CompilerParams(
            collective_id=0, has_side_effects=True, vmem_limit_bytes=56 * 1024 * 1024),
    )(volumes[0], depth_shift.reshape(1), plane_shift.reshape(2), fraction_steps.reshape(3))
    return velocity[None], template


def solution(mesh):
    return jax.shard_map(
        shards,
        mesh=mesh,
        in_specs=(
            P("subj", "depth", None, None),
            P("subj", "depth"),
            P("subj", "depth", None),
            P("subj", "depth", None),
        ),
        out_specs=(P("subj", None, "depth", None, None), P("depth", None, None)),
        check_vma=False,
    )
```

```python
import math

import jax
import jax.numpy as jnp
from jax import lax
from jax.experimental import pallas as pl
from jax.experimental.pallas import tpu as pltpu
from jax.sharding import PartitionSpec as P

MESH = pl.DeviceIdType.MESH
F32, BF16 = jnp.float32, jnp.bfloat16
H = W = 256
B = 8
HALO = 6
NE = B + 2 * HALO
PAD = 16
EPS = 1e-5
SRC = (0, 48, 96, 144, 192, 240, 256)
C = len(SRC) - 1


def lagging(ends):
    return tuple(max(e - 16, 0) if e < H else H for e in ends)


WE = lagging(SRC)
FE = lagging(WE)
GE = lagging(FE)
NF = max(FE[i + 1] - FE[i] for i in range(C))
G = 16
U = 4

SRC_R, SRC_L, W_R, W_L, W_C, S_Z, T_C, T_R, T_L, R_L, R_R = range(11)


def taps():
    raw = [math.exp(-(t * t) / 4.5) for t in range(-4, 5)]
    total = sum(raw)
    return [r / total for r in raw]


def iota(shape, dim):
    return lax.broadcasted_iota(jnp.int32, shape, dim)


def gauss_matrix(rows, cols, shift):
    away = jnp.abs(iota((rows, cols), 0) + shift - iota((rows, cols), 1))
    w = taps()
    out = jnp.zeros((rows, cols), F32)
    for t in range(5):
        out = jnp.where(away == t, F32(w[4 + t]), out)
    return out.astype(BF16)


def dot(a, b):
    return jnp.dot(a, b, preferred_element_type=F32)


def rounded_gain():
    import numpy as np
    import ml_dtypes
    w = np.array(taps(), np.float32)
    return float(w.sum()) / float(w.astype(ml_dtypes.bfloat16).astype(np.float32).sum())


def kernel(vol, dsh, psh, fst, vel, tmpl, *refs):
    ext = refs[:C]
    (iext, text, wp, sb, sz, yb, gy, sp, bq, gxs, fo, zs, vst, ax2, bx3, dx, gx, ssem, rsem, lsem) = refs[C:]
    me, d = lax.axis_index("subj"), lax.axis_index("depth")
    nd = lax.axis_size("depth")
    core = lax.rem(me, 2)
    mate = me + 1 - 2 * core
    far = lax.rem(me + 2, 4)
    right, left = lax.rem(d + 1, nd), lax.rem(d + nd - 1, nd)
    has_l, has_r = d > 0, d < nd - 1

    def remote(src, dst, p, kind, subj, depth):
        return pltpu.make_async_remote_copy(
            src_ref=src, dst_ref=dst, send_sem=ssem.at[p, kind], recv_sem=rsem.at[p, kind],
            device_id={"subj": subj, "depth": depth}, device_id_type=MESH)

    barrier = pltpu.get_barrier_semaphore()

    def greet(subj, depth):
        pl.semaphore_signal(barrier, inc=1, device_id={"subj": subj, "depth": depth}, device_id_type=MESH)

    greet(mate, d)
    greet(far, d)

    @pl.when(has_l)
    def _():
        greet(me, left)

    @pl.when(has_r)
    def _():
        greet(me, right)

    mine = pl.ds(pl.multiple_of(core * 128, 128), 128)
    other = pl.ds(pl.multiple_of((1 - core) * 128, 128), 128)

    def rows_of(ends, p):
        return pl.ds(ends[p], ends[p + 1] - ends[p])

    def padded_rows(ends, p):
        return pl.ds(PAD + ends[p], ends[p + 1] - ends[p])

    def copy_of(p, kind):
        if kind == SRC_R:
            return remote(vol.at[:, rows_of(SRC, p), :], ext[p].at[0:B], p, kind, me, right)
        if kind == SRC_L:
            return remote(vol.at[:, rows_of(SRC, p), :], ext[p].at[2 * B:3 * B], p, kind, me, left)
        r, q = rows_of(WE, p), padded_rows(WE, p)
        if kind == W_R:
            return remote(iext.at[B:B + HALO, q, :], iext.at[0:HALO, q, :], p, kind, me, right)
        if kind == W_L:
            return remote(iext.at[HALO:2 * HALO, q, :], iext.at[B + HALO:NE, q, :], p, kind, me, left)
        if kind == W_C:
            return remote(iext.at[HALO:HALO + B, q, other], wp.at[:, r, :], p, kind, mate, d)
        if kind == S_Z:
            return remote(sb.at[:, r, :], sz.at[:, r, :], p, kind, far, d)
        if kind == T_C:
            part = text.at[HALO:HALO + B, q, mine]
            return remote(part, part, p, kind, mate, d)
        if kind == T_R:
            return remote(text.at[B:B + HALO, q, mine], text.at[0:HALO, q, mine], p, kind, me, right)
        if kind == T_L:
            return remote(text.at[HALO:2 * HALO, q, mine], text.at[B + HALO:NE, q, mine], p, kind, me, left)
        part = text.at[0:HALO, q, mine] if kind == R_L else text.at[B + HALO:NE, q, mine]
        return remote(part, part, p, kind, mate, d)

    sends = {SRC_R: has_r, W_R: has_r, T_R: has_r, SRC_L: has_l, W_L: has_l, T_L: has_l, R_L: has_l, R_R: has_r}
    gets = {SRC_R: has_l, W_R: has_l, T_R: has_l, SRC_L: has_r, W_L: has_r, T_L: has_r, R_L: has_l, R_R: has_r}

    def start(p, *kinds):
        for kind in kinds:
            if kind in sends:
                pl.when(sends[kind])(lambda kind=kind: copy_of(p, kind).start())
            else:
                copy_of(p, kind).start()

    def landed(p, *kinds):
        for kind in kinds:
            if kind in gets:
                pl.when(gets[kind])(lambda kind=kind: copy_of(p, kind).wait_recv())
            else:
                copy_of(p, kind).wait_recv()

    def own_copy(p):
        return pltpu.make_async_copy(vol.at[:, rows_of(SRC, p), :], ext[p].at[B:2 * B], lsem.at[p])

    for p in range(C):
        own_copy(p).start()

    pl.semaphore_wait(barrier, 2 + has_l.astype(jnp.int32) + has_r.astype(jnp.int32))
    for p in range(C):
        start(p, SRC_R, SRC_L)

    dz, dy, dxs = dsh[0], psh[0], psh[1]
    fz, fy, fx = fst[0].astype(F32) * 0.25, fst[1].astype(F32) * 0.25, fst[2].astype(F32) * 0.25

    def zero_pads(ref, count):
        zero = jnp.zeros((PAD, W), BF16)

        def body(z, carry):
            ref[z, 0:PAD, :] = zero
            ref[z, PAD + H:2 * PAD + H, :] = zero
            return carry
        lax.fori_loop(0, count, body, 0)

    zero_pads(iext, NE)
    zero_pads(text, NE)
    for k in range(3):
        zero_pads(zs.at[k], B)

    def zero_planes(lo):
        def body(z, carry):
            zero = jnp.zeros((H, W), BF16)
            iext[lo + z, PAD:PAD + H, :] = zero
            text[lo + z, PAD:PAD + H, :] = zero
            return carry
        lax.fori_loop(0, HALO, body, 0)

    @pl.when(d == 0)
    def _():
        zero_planes(0)
        for p in range(C):
            ext[p][0:B] = jnp.zeros((B,) + ext[p].shape[1:], BF16)

    @pl.when(d == nd - 1)
    def _():
        zero_planes(B + HALO)
        for p in range(C):
            ext[p][2 * B:3 * B] = jnp.zeros((B,) + ext[p].shape[1:], BF16)

    row, col = iota((W, W), 0), iota((W, W), 1)
    a_x = jnp.where(row == col + dxs, 1.0 - fx, jnp.where(row == col + dxs + 1, fx, 0.0)).astype(BF16)
    ax2[0:W, :] = a_x
    ax2[W:2 * W, :] = a_x
    b_x = jnp.where(jnp.abs(row - col) <= 2, 1.0, 0.0).astype(BF16)
    for i in range(3):
        bx3[i * W:(i + 1) * W, :] = b_x
    dx[...] = jnp.where(row == col + 1, 0.5, jnp.where(row == col - 1, -0.5, 0.0)).astype(BF16)
    gx[...] = gauss_matrix(W, W, 0)

    def warp(p):
        a, n = WE[p], WE[p + 1] - WE[p]
        ka = 0 if p == 0 else SRC[p] - 32
        k = SRC[p + 1] - ka
        at, j = iota((n, 2 * k), 0) + (a + dy), iota((n, 2 * k), 1)
        w_z = jnp.where(j < k, 1.0 - fz, fz)
        j = jnp.where(j < k, j, j - k) + ka
        a_y = (w_z * jnp.where(j == at, 1.0 - fy, jnp.where(j == at + 1, fy, 0.0))).astype(BF16)

        for half in range(0, B, U):
            split = []
            for z in range(half, half + U):
                parts = []
                for c in range(2):
                    if p > 0:
                        size = SRC[p] - SRC[p - 1]
                        parts.append(ext[p - 1][8 + dz + z + c, size - 32:size, :])
                    parts.append(ext[p][8 + dz + z + c])
                r = dot(a_y, jnp.concatenate(parts, 0))
                hi = r.astype(BF16)
                lo = (r - hi.astype(F32)).astype(BF16)
                split.append(jnp.concatenate([hi, lo], 1))
            out = dot(jnp.concatenate(split, 0), ax2[...]).astype(BF16)
            iext[HALO + half:HALO + half + U, PAD + a:PAD + a + n, :] = out.reshape(U, n, W)

    def partial_sum(p):
        r, q = rows_of(WE, p), padded_rows(WE, p)

        def body(z, carry):
            sb[z, r, :] = (iext[HALO + z, q, mine].astype(F32) + wp[z, r, :].astype(F32)).astype(BF16)
            return carry
        lax.fori_loop(0, B, body, 0)

    def template(p):
        r, q = rows_of(WE, p), padded_rows(WE, p)

        def body(z, carry):
            text[HALO + z, q, mine] = ((sb[z, r, :].astype(F32) + sz[z, r, :].astype(F32)) * 0.25).astype(BF16)
            return carry
        lax.fori_loop(0, B, body, 0)

    def force(p):
        a, n = FE[p], FE[p + 1] - FE[p]
        k = n + 2 * PAD
        away = iota((n, k), 0) + PAD - iota((n, k), 1)
        b_y = jnp.where(jnp.abs(away) <= 2, 1.0, 0.0).astype(BF16)
        d_y = jnp.where(away == -1, 0.5, jnp.where(away == 1, -0.5, 0.0)).astype(BF16)
        bd = jnp.concatenate([b_y, d_y], 0)
        b2 = jnp.concatenate([b_y, b_y], 1)

        def in_rows(z):
            i, j = iext[z, a:a + k, :], text[z, a:a + k, :]
            both = dot(bd, i)
            yb[0, z, 0:n, :] = both[:n]
            gy[z, 0:n, :] = both[n:]
            yb[1, z, 0:n, :] = dot(b_y, j)
            fi, fj = i.astype(F32), j.astype(F32)
            for q, v in ((2, fi * fj), (3, fi * fi), (4, fj * fj)):
                hi = v.astype(BF16)
                lo = (v - hi.astype(F32)).astype(BF16)
                yb[q, z, 0:n, :] = dot(b2, jnp.concatenate([hi, lo], 0))

        def in_rows_of(zu, carry):
            for u in range(U):
                in_rows(zu * U + u)
            return carry
        lax.fori_loop(0, NE // U, in_rows_of, 0)

        def planes(zu, carry):
            z0 = zu * U
            for q in range(5):
                for g in range(0, n, G):
                    v = [yb[q, z0 + t, g:g + G, :] for t in range(8)]
                    m12, m34, m56 = v[1] + v[2], v[3] + v[4], v[5] + v[6]
                    low, high = m12 + m34, m34 + m56
                    for u, s in enumerate((v[0] + low, low + v[5], v[2] + high, high + v[7])):
                        at = (u * 5 + q) * n + g
                        for part in range(3):
                            piece = s.astype(BF16)
                            sp[at:at + G, part * W:(part + 1) * W] = piece
                            if part < 2:
                                s = s - piece.astype(F32)
            bq[0:5 * U * n, :] = dot(sp[0:5 * U * n, :], bx3[...])
            gxs[0:U * n, :] = dot(iext[pl.ds(z0 + 2, U), PAD + a:PAD + a + n, :].reshape(U * n, W), dx[...])
            for u in range(U):
                z = z0 + u
                whole = (d * B - 4 + z >= 0) & (d * B - 4 + z < nd * B)
                for g in range(0, n, G):
                    here = slice(PAD + a + g, PAD + a + g + G)
                    b_i, b_j, b_ij, b_ii, b_jj = (
                        bq[(u * 5 + q) * n + g:(u * 5 + q) * n + g + G, :] * (1 / 125) for q in range(5))
                    cov = b_ij - b_i * b_j
                    v_i = b_ii - b_i * b_i + EPS
                    v_j = b_jj - b_j * b_j + EPS
                    scaled = cov / (v_i * v_j)
                    i, j = iext[z + 2, here, :].astype(F32), text[z + 2, here, :].astype(F32)
                    common = 2.0 * scaled * ((j - b_j) - scaled * v_j * (i - b_i))
                    common = jnp.where(whole, common, 0.0)
                    g_z = (iext[z + 3, here, :].astype(F32) - iext[z + 1, here, :].astype(F32)) * 0.5
                    fo[0, z, g:g + G, :] = (common * g_z).astype(BF16)
                    fo[1, z, g:g + G, :] = (common * gy[z + 2, g:g + G, :]).astype(BF16)
                    fo[2, z, g:g + G, :] = (common * gxs[u * n + g:u * n + g + G, :]).astype(BF16)
            return carry
        lax.fori_loop(0, 2 * B // U, planes, 0)

        w = [8.0 * rounded_gain() ** 2 * t for t in taps()]

        def along_depth(g, carry):
            r = pl.ds(pl.multiple_of(g * G, G), G)
            out = pl.ds(pl.multiple_of(PAD + a + g * G, G), G)
            for k3 in range(3):
                for half in range(2):
                    lanes = slice(half * 128, half * 128 + 128)
                    f = [fo[k3, z, r, lanes].astype(F32) for z in range(2 * B)]
                    for z in range(B):
                        s = f[z + 4] * w[4]
                        for t in range(1, 5):
                            s = s + (f[z + 4 - t] + f[z + 4 + t]) * w[4 + t]
                        zs[k3, z, out, lanes] = s.astype(BF16)
            return carry
        lax.fori_loop(0, n // G, along_depth, 0)

    def out_copy(p):
        r = rows_of(GE, p)
        return pltpu.make_async_copy(vst.at[:, :, r, :], vel.at[:, :, r, :], lsem.at[C + p])

    def smooth(p):
        a, n = GE[p], GE[p + 1] - GE[p]
        if n == 0:
            return
        g_y = gauss_matrix(n, n + 2 * PAD, PAD)

        for k3 in range(3):
            for z in range(0, B, U):
                r = [dot(g_y, zs[k3, z + u, a:a + n + 2 * PAD, :]).astype(BF16) for u in range(U)]
                out = dot(jnp.concatenate(r, 0), gx[...]).astype(BF16)
                vst[k3, z:z + U, a:a + n, :] = out.reshape(U, n, W)
        out_copy(p).start()

    whole_template = pltpu.make_async_copy(
        text.at[HALO:HALO + B, PAD:PAD + H, :], tmpl, lsem.at[2 * C])
    for step, p in (
            ('s', 0),
            ('c', 0),
            ('w', 0),
            ('s', 1),
            ('c', 1),
            ('w', 1),
            ('t', 0),
            ('s', 2),
            ('c', 2),
            ('w', 2),
            ('t', 1),
            ('r', 0),
            ('f', 0),
            ('s', 3),
            ('c', 3),
            ('w', 3),
            ('t', 2),
            ('r', 1),
            ('f', 1),
            ('s', 4),
            ('c', 4),
            ('w', 4),
            ('t', 3),
            ('r', 2),
            ('f', 2),
            ('s', 5),
            ('c', 5),
            ('w', 5),
            ('t', 4),
            ('r', 3),
            ('f', 3),
            ('t', 5),
            ('r', 4),
            ('f', 4),
            ('r', 5),
            ('f', 5)):
        if step == "s":
            own_copy(p).wait()
            landed(p, SRC_R, SRC_L)
            warp(p)
            start(p, W_C)
        elif step == "c":
            landed(p, W_C)
            partial_sum(p)
            start(p, S_Z)
        elif step == "w":
            start(p, W_R, W_L)
        elif step == "t":
            landed(p, S_Z)
            template(p)
            start(p, T_R, T_L, T_C)
        elif step == "r":
            landed(p, T_R, T_L)
            start(p, R_L, R_R)
        elif step == "f":
            landed(p, W_R, W_L, T_C, R_L, R_R)
            if p == C - 1:
                whole_template.start()
            force(p)
            smooth(p)

    for p in range(C):
        if GE[p + 1] > GE[p]:
            out_copy(p).wait()
    whole_template.wait()
    for p in range(C):
        for kind in range(11):
            if kind in sends:
                pl.when(sends[kind])(lambda kind=kind: copy_of(p, kind).wait_send())
            else:
                copy_of(p, kind).wait_send()


def shards(volumes, depth_shift, plane_shift, fraction_steps):
    smem = pl.BlockSpec(memory_space=pltpu.SMEM)
    anywhere = pl.BlockSpec(memory_space=pl.ANY)
    scratch = [pltpu.VMEM((3 * B, SRC[p + 1] - SRC[p], W), BF16) for p in range(C)]
    scratch += [
        pltpu.VMEM((NE, H + 2 * PAD, W), BF16),
        pltpu.VMEM((NE, H + 2 * PAD, W), BF16),
        pltpu.VMEM((B, H, 128), BF16),
        pltpu.VMEM((B, H, 128), BF16),
        pltpu.VMEM((B, H, 128), BF16),
        pltpu.VMEM((5, NE, NF, W), F32),
        pltpu.VMEM((NE, NF, W), F32),
        pltpu.VMEM((5 * U * NF, 3 * W), BF16),
        pltpu.VMEM((5 * U * NF, W), F32),
        pltpu.VMEM((U * NF, W), F32),
        pltpu.VMEM((3, 2 * B, NF, W), BF16),
        pltpu.VMEM((3, B, H + 2 * PAD, W), BF16),
        pltpu.VMEM((3, B, H, W), BF16),
        pltpu.VMEM((2 * W, W), BF16),
        pltpu.VMEM((3 * W, W), BF16),
        pltpu.VMEM((W, W), BF16),
        pltpu.VMEM((W, W), BF16),
        pltpu.SemaphoreType.DMA((C, 11)),
        pltpu.SemaphoreType.DMA((C, 11)),
        pltpu.SemaphoreType.DMA((2 * C + 1,)),
    ]
    velocity, template = pl.pallas_call(
        kernel,
        out_shape=(jax.ShapeDtypeStruct((3, B, H, W), BF16), jax.ShapeDtypeStruct((B, H, W), BF16)),
        in_specs=[anywhere, smem, smem, smem],
        out_specs=(anywhere, anywhere),
        scratch_shapes=scratch,
        compiler_params=pltpu.CompilerParams(
            collective_id=0, has_side_effects=True, vmem_limit_bytes=56 * 1024 * 1024),
    )(volumes[0], depth_shift.reshape(1), plane_shift.reshape(2), fraction_steps.reshape(3))
    return velocity[None], template


def solution(mesh):
    return jax.shard_map(
        shards,
        mesh=mesh,
        in_specs=(
            P("subj", "depth", None, None),
            P("subj", "depth"),
            P("subj", "depth", None),
            P("subj", "depth", None),
        ),
        out_specs=(P("subj", None, "depth", None, None), P("depth", None, None)),
        check_vma=False,
    )
```

```python
import math

import jax
import jax.numpy as jnp
from jax import lax
from jax.experimental import pallas as pl
from jax.experimental.pallas import tpu as pltpu
from jax.sharding import PartitionSpec as P

MESH = pl.DeviceIdType.MESH
F32, BF16 = jnp.float32, jnp.bfloat16
H = W = 256
B = 8
HALO = 6
NE = B + 2 * HALO
PAD = 16
EPS = 1e-5
SRC = (0, 48, 96, 144, 192, 240, 256)
C = len(SRC) - 1


def lagging(ends):
    return tuple(max(e - 16, 0) if e < H else H for e in ends)


WE = lagging(SRC)
FE = lagging(WE)
NF = max(FE[i + 1] - FE[i] for i in range(C))
G = 16
U = 4
Z = 4

SRC_R, SRC_L, W_R, W_L, W_C, S_Z, T_C, T_R, T_L, R_L, R_R = range(11)


def taps():
    raw = [math.exp(-(t * t) / 4.5) for t in range(-4, 5)]
    total = sum(raw)
    return [r / total for r in raw]


def iota(shape, dim):
    return lax.broadcasted_iota(jnp.int32, shape, dim)


def gauss_matrix(rows, cols, shift):
    away = jnp.abs(iota((rows, cols), 0) + shift - iota((rows, cols), 1))
    w = taps()
    out = jnp.zeros((rows, cols), F32)
    for t in range(5):
        out = jnp.where(away == t, F32(w[4 + t]), out)
    return out.astype(BF16)


def dot(a, b):
    return jnp.dot(a, b, preferred_element_type=F32)


def rounded_gain():
    import numpy as np
    import ml_dtypes
    w = np.array(taps(), np.float32)
    return float(w.sum()) / float(w.astype(ml_dtypes.bfloat16).astype(np.float32).sum())


def kernel(vol, dsh, psh, fst, zs_out, tmpl, *refs):
    ext = refs[:C]
    (iext, text, wp, sb, sz, yb, gy, sp, bq, gxs, fo, zs, ax2, bx3, dx, ssem, rsem, lsem) = refs[C:]
    me, d = lax.axis_index("subj"), lax.axis_index("depth")
    nd = lax.axis_size("depth")
    core = lax.rem(me, 2)
    mate = me + 1 - 2 * core
    far = lax.rem(me + 2, 4)
    right, left = lax.rem(d + 1, nd), lax.rem(d + nd - 1, nd)
    has_l, has_r = d > 0, d < nd - 1

    def remote(src, dst, p, kind, subj, depth):
        return pltpu.make_async_remote_copy(
            src_ref=src, dst_ref=dst, send_sem=ssem.at[p, kind], recv_sem=rsem.at[p, kind],
            device_id={"subj": subj, "depth": depth}, device_id_type=MESH)

    barrier = pltpu.get_barrier_semaphore()

    def greet(subj, depth):
        pl.semaphore_signal(barrier, inc=1, device_id={"subj": subj, "depth": depth}, device_id_type=MESH)

    greet(mate, d)
    greet(far, d)

    @pl.when(has_l)
    def _():
        greet(me, left)

    @pl.when(has_r)
    def _():
        greet(me, right)

    mine = pl.ds(pl.multiple_of(core * 128, 128), 128)
    other = pl.ds(pl.multiple_of((1 - core) * 128, 128), 128)

    def rows_of(ends, p):
        return pl.ds(ends[p], ends[p + 1] - ends[p])

    def padded_rows(ends, p):
        return pl.ds(PAD + ends[p], ends[p + 1] - ends[p])

    def copy_of(p, kind):
        if kind == SRC_R:
            return remote(vol.at[:, rows_of(SRC, p), :], ext[p].at[0:B], p, kind, me, right)
        if kind == SRC_L:
            return remote(vol.at[:, rows_of(SRC, p), :], ext[p].at[2 * B:3 * B], p, kind, me, left)
        r, q = rows_of(WE, p), padded_rows(WE, p)
        if kind == W_R:
            return remote(iext.at[B:B + HALO, q, :], iext.at[0:HALO, q, :], p, kind, me, right)
        if kind == W_L:
            return remote(iext.at[HALO:2 * HALO, q, :], iext.at[B + HALO:NE, q, :], p, kind, me, left)
        if kind == W_C:
            return remote(iext.at[HALO:HALO + B, q, other], wp.at[:, r, :], p, kind, mate, d)
        if kind == S_Z:
            return remote(sb.at[:, r, :], sz.at[:, r, :], p, kind, far, d)
        if kind == T_C:
            part = text.at[HALO:HALO + B, q, mine]
            return remote(part, part, p, kind, mate, d)
        if kind == T_R:
            return remote(text.at[B:B + HALO, q, mine], text.at[0:HALO, q, mine], p, kind, me, right)
        if kind == T_L:
            return remote(text.at[HALO:2 * HALO, q, mine], text.at[B + HALO:NE, q, mine], p, kind, me, left)
        part = text.at[0:HALO, q, mine] if kind == R_L else text.at[B + HALO:NE, q, mine]
        return remote(part, part, p, kind, mate, d)

    sends = {SRC_R: has_r, W_R: has_r, T_R: has_r, SRC_L: has_l, W_L: has_l, T_L: has_l, R_L: has_l, R_R: has_r}
    gets = {SRC_R: has_l, W_R: has_l, T_R: has_l, SRC_L: has_r, W_L: has_r, T_L: has_r, R_L: has_l, R_R: has_r}

    def start(p, *kinds):
        for kind in kinds:
            if kind in sends:
                pl.when(sends[kind])(lambda kind=kind: copy_of(p, kind).start())
            else:
                copy_of(p, kind).start()

    def landed(p, *kinds):
        for kind in kinds:
            if kind in gets:
                pl.when(gets[kind])(lambda kind=kind: copy_of(p, kind).wait_recv())
            else:
                copy_of(p, kind).wait_recv()

    def own_copy(p):
        return pltpu.make_async_copy(vol.at[:, rows_of(SRC, p), :], ext[p].at[B:2 * B], lsem.at[p])

    for p in range(C):
        own_copy(p).start()

    pl.semaphore_wait(barrier, 2 + has_l.astype(jnp.int32) + has_r.astype(jnp.int32))
    for p in range(C):
        start(p, SRC_R, SRC_L)

    dz, dy, dxs = dsh[0], psh[0], psh[1]
    fz, fy, fx = fst[0].astype(F32) * 0.25, fst[1].astype(F32) * 0.25, fst[2].astype(F32) * 0.25

    def zero_pads(ref, count):
        zero = jnp.zeros((PAD, W), BF16)

        def body(z, carry):
            ref[z, 0:PAD, :] = zero
            ref[z, PAD + H:2 * PAD + H, :] = zero
            return carry
        lax.fori_loop(0, count, body, 0)

    zero_pads(iext, NE)
    zero_pads(text, NE)

    def zero_planes(lo):
        def body(z, carry):
            zero = jnp.zeros((H, W), BF16)
            iext[lo + z, PAD:PAD + H, :] = zero
            text[lo + z, PAD:PAD + H, :] = zero
            return carry
        lax.fori_loop(0, HALO, body, 0)

    @pl.when(d == 0)
    def _():
        zero_planes(0)
        for p in range(C):
            ext[p][0:B] = jnp.zeros((B,) + ext[p].shape[1:], BF16)

    @pl.when(d == nd - 1)
    def _():
        zero_planes(B + HALO)
        for p in range(C):
            ext[p][2 * B:3 * B] = jnp.zeros((B,) + ext[p].shape[1:], BF16)

    row, col = iota((W, W), 0), iota((W, W), 1)
    a_x = jnp.where(row == col + dxs, 1.0 - fx, jnp.where(row == col + dxs + 1, fx, 0.0)).astype(BF16)
    ax2[0:W, :] = a_x
    ax2[W:2 * W, :] = a_x
    b_x = jnp.where(jnp.abs(row - col) <= 2, 1.0, 0.0).astype(BF16)
    for i in range(3):
        bx3[i * W:(i + 1) * W, :] = b_x
    dx[...] = jnp.where(row == col + 1, 0.5, jnp.where(row == col - 1, -0.5, 0.0)).astype(BF16)

    def warp(p):
        a, n = WE[p], WE[p + 1] - WE[p]
        ka = 0 if p == 0 else SRC[p] - 32
        k = SRC[p + 1] - ka
        at, j = iota((n, 2 * k), 0) + (a + dy), iota((n, 2 * k), 1)
        w_z = jnp.where(j < k, 1.0 - fz, fz)
        j = jnp.where(j < k, j, j - k) + ka
        a_y = (w_z * jnp.where(j == at, 1.0 - fy, jnp.where(j == at + 1, fy, 0.0))).astype(BF16)

        for half in range(0, B, U):
            split = []
            for z in range(half, half + U):
                parts = []
                for c in range(2):
                    if p > 0:
                        size = SRC[p] - SRC[p - 1]
                        parts.append(ext[p - 1][8 + dz + z + c, size - 32:size, :])
                    parts.append(ext[p][8 + dz + z + c])
                r = dot(a_y, jnp.concatenate(parts, 0))
                hi = r.astype(BF16)
                lo = (r - hi.astype(F32)).astype(BF16)
                split.append(jnp.concatenate([hi, lo], 1))
            out = dot(jnp.concatenate(split, 0), ax2[...]).astype(BF16)
            iext[HALO + half:HALO + half + U, PAD + a:PAD + a + n, :] = out.reshape(U, n, W)

    def partial_sum(p):
        r, q = rows_of(WE, p), padded_rows(WE, p)

        def body(z, carry):
            sb[z, r, :] = (iext[HALO + z, q, mine].astype(F32) + wp[z, r, :].astype(F32)).astype(BF16)
            return carry
        lax.fori_loop(0, B, body, 0)

    def template(p):
        r, q = rows_of(WE, p), padded_rows(WE, p)

        def body(z, carry):
            text[HALO + z, q, mine] = ((sb[z, r, :].astype(F32) + sz[z, r, :].astype(F32)) * 0.25).astype(BF16)
            return carry
        lax.fori_loop(0, B, body, 0)

    def force(p):
        a, n = FE[p], FE[p + 1] - FE[p]
        k = n + 2 * PAD
        away = iota((n, k), 0) + PAD - iota((n, k), 1)
        b_y = jnp.where(jnp.abs(away) <= 2, 1.0, 0.0).astype(BF16)
        d_y = jnp.where(away == -1, 0.5, jnp.where(away == 1, -0.5, 0.0)).astype(BF16)
        bd = jnp.concatenate([b_y, d_y], 0)
        b2 = jnp.concatenate([b_y, b_y], 1)

        def in_rows(z):
            i, j = iext[z, a:a + k, :], text[z, a:a + k, :]
            both = dot(bd, i)
            yb[0, z, 0:n, :] = both[:n]
            gy[z, 0:n, :] = both[n:]
            yb[1, z, 0:n, :] = dot(b_y, j)
            fi, fj = i.astype(F32), j.astype(F32)
            for q, v in ((2, fi * fj), (3, fi * fi), (4, fj * fj)):
                hi = v.astype(BF16)
                lo = (v - hi.astype(F32)).astype(BF16)
                yb[q, z, 0:n, :] = dot(b2, jnp.concatenate([hi, lo], 0))

        def in_rows_of(zu, carry):
            for u in range(U):
                in_rows(zu * U + u)
            return carry
        lax.fori_loop(0, NE // U, in_rows_of, 0)

        def planes(zu, carry):
            z0 = zu * U
            for q in range(5):
                for g in range(0, n, G):
                    v = [yb[q, z0 + t, g:g + G, :] for t in range(8)]
                    m12, m34, m56 = v[1] + v[2], v[3] + v[4], v[5] + v[6]
                    low, high = m12 + m34, m34 + m56
                    for u, s in enumerate((v[0] + low, low + v[5], v[2] + high, high + v[7])):
                        at = (u * 5 + q) * n + g
                        for part in range(3):
                            piece = s.astype(BF16)
                            sp[at:at + G, part * W:(part + 1) * W] = piece
                            if part < 2:
                                s = s - piece.astype(F32)
            bq[0:5 * U * n, :] = dot(sp[0:5 * U * n, :], bx3[...])
            gxs[0:U * n, :] = dot(iext[pl.ds(z0 + 2, U), PAD + a:PAD + a + n, :].reshape(U * n, W), dx[...])
            for u in range(U):
                z = z0 + u
                whole = (d * B - 4 + z >= 0) & (d * B - 4 + z < nd * B)
                for g in range(0, n, G):
                    here = slice(PAD + a + g, PAD + a + g + G)
                    b_i, b_j, b_ij, b_ii, b_jj = (
                        bq[(u * 5 + q) * n + g:(u * 5 + q) * n + g + G, :] * (1 / 125) for q in range(5))
                    cov = b_ij - b_i * b_j
                    v_i = b_ii - b_i * b_i + EPS
                    v_j = b_jj - b_j * b_j + EPS
                    scaled = cov / (v_i * v_j)
                    i, j = iext[z + 2, here, :].astype(F32), text[z + 2, here, :].astype(F32)
                    common = 2.0 * scaled * ((j - b_j) - scaled * v_j * (i - b_i))
                    common = jnp.where(whole, common, 0.0)
                    g_z = (iext[z + 3, here, :].astype(F32) - iext[z + 1, here, :].astype(F32)) * 0.5
                    fo[0, z, g:g + G, :] = (common * g_z).astype(BF16)
                    fo[1, z, g:g + G, :] = (common * gy[z + 2, g:g + G, :]).astype(BF16)
                    fo[2, z, g:g + G, :] = (common * gxs[u * n + g:u * n + g + G, :]).astype(BF16)
            return carry
        lax.fori_loop(0, 2 * B // U, planes, 0)

        w = [8.0 * rounded_gain() ** 2 * t for t in taps()]

        def along_depth(g, carry):
            r = pl.ds(pl.multiple_of(g * G, G), G)
            out = pl.ds(pl.multiple_of(a + g * G, G), G)
            for k3 in range(3):
                for half in range(2):
                    lanes = slice(half * 128, half * 128 + 128)
                    f = [fo[k3, z, r, lanes].astype(F32) for z in range(2 * B)]
                    for z in range(B):
                        s = f[z + 4] * w[4]
                        for t in range(1, 5):
                            s = s + (f[z + 4 - t] + f[z + 4 + t]) * w[4 + t]
                        zs[k3, z, out, lanes] = s.astype(BF16)
            return carry
        lax.fori_loop(0, n // G, along_depth, 0)

    def out_copy(p):
        r = rows_of(FE, p)
        return pltpu.make_async_copy(zs.at[:, :, r, :], zs_out.at[:, :, r, :], lsem.at[C + p])

    whole_template = pltpu.make_async_copy(
        text.at[HALO:HALO + B, PAD:PAD + H, :], tmpl, lsem.at[2 * C])
    for step, p in (
            ('s', 0),
            ('c', 0),
            ('w', 0),
            ('s', 1),
            ('c', 1),
            ('w', 1),
            ('t', 0),
            ('s', 2),
            ('c', 2),
            ('w', 2),
            ('r', 0),
            ('t', 1),
            ('f', 0),
            ('s', 3),
            ('c', 3),
            ('w', 3),
            ('r', 1),
            ('t', 2),
            ('f', 1),
            ('s', 4),
            ('c', 4),
            ('w', 4),
            ('r', 2),
            ('t', 3),
            ('f', 2),
            ('s', 5),
            ('c', 5),
            ('w', 5),
            ('r', 3),
            ('t', 4),
            ('f', 3),
            ('r', 4),
            ('t', 5),
            ('f', 4),
            ('r', 5),
            ('f', 5)):
        if step == "s":
            own_copy(p).wait()
            landed(p, SRC_R, SRC_L)
            warp(p)
            start(p, W_C)
        elif step == "c":
            landed(p, W_C)
            partial_sum(p)
            start(p, S_Z)
        elif step == "w":
            start(p, W_R, W_L)
        elif step == "t":
            landed(p, S_Z)
            template(p)
            start(p, T_R, T_L, T_C)
        elif step == "r":
            landed(p, T_R, T_L)
            start(p, R_L, R_R)
        elif step == "f":
            landed(p, W_R, W_L, T_C, R_L, R_R)
            if p == C - 1:
                whole_template.start()
            force(p)
            out_copy(p).start()

    for p in range(C):
        out_copy(p).wait()
    whole_template.wait()
    for p in range(C):
        for kind in range(11):
            if kind in sends:
                pl.when(sends[kind])(lambda kind=kind: copy_of(p, kind).wait_send())
            else:
                copy_of(p, kind).wait_send()


def smooth_in_plane(along, averaged, velocity, template, g):
    @pl.when(pl.program_id(0) == 0)
    def _():
        g[...] = gauss_matrix(W, W, 0)

    r = [dot(g[...], along[k3, z]).astype(BF16) for k3 in range(3) for z in range(Z)]
    out = dot(jnp.concatenate(r, 0), g[...]).astype(BF16)
    velocity[...] = out.reshape(3, Z, H, W)
    template[...] = averaged[...]


def shards(volumes, depth_shift, plane_shift, fraction_steps):
    smem = pl.BlockSpec(memory_space=pltpu.SMEM)
    anywhere = pl.BlockSpec(memory_space=pl.ANY)
    scratch = [pltpu.VMEM((3 * B, SRC[p + 1] - SRC[p], W), BF16) for p in range(C)]
    scratch += [
        pltpu.VMEM((NE, H + 2 * PAD, W), BF16),
        pltpu.VMEM((NE, H + 2 * PAD, W), BF16),
        pltpu.VMEM((B, H, 128), BF16),
        pltpu.VMEM((B, H, 128), BF16),
        pltpu.VMEM((B, H, 128), BF16),
        pltpu.VMEM((5, NE, NF, W), F32),
        pltpu.VMEM((NE, NF, W), F32),
        pltpu.VMEM((5 * U * NF, 3 * W), BF16),
        pltpu.VMEM((5 * U * NF, W), F32),
        pltpu.VMEM((U * NF, W), F32),
        pltpu.VMEM((3, 2 * B, NF, W), BF16),
        pltpu.VMEM((3, B, H, W), BF16),
        pltpu.VMEM((2 * W, W), BF16),
        pltpu.VMEM((3 * W, W), BF16),
        pltpu.VMEM((W, W), BF16),
        pltpu.SemaphoreType.DMA((C, 11)),
        pltpu.SemaphoreType.DMA((C, 11)),
        pltpu.SemaphoreType.DMA((2 * C + 1,)),
    ]
    along, averaged = pl.pallas_call(
        kernel,
        out_shape=(jax.ShapeDtypeStruct((3, B, H, W), BF16), jax.ShapeDtypeStruct((B, H, W), BF16)),
        in_specs=[anywhere, smem, smem, smem],
        out_specs=(anywhere, anywhere),
        scratch_shapes=scratch,
        compiler_params=pltpu.CompilerParams(
            collective_id=0, has_side_effects=True, vmem_limit_bytes=56 * 1024 * 1024),
    )(volumes[0], depth_shift.reshape(1), plane_shift.reshape(2), fraction_steps.reshape(3))
    three = pl.BlockSpec((3, Z, H, W), lambda z: (0, z, 0, 0))
    one = pl.BlockSpec((Z, H, W), lambda z: (z, 0, 0))
    velocity, template = pl.pallas_call(
        smooth_in_plane,
        grid=(B // Z,),
        out_shape=(jax.ShapeDtypeStruct((3, B, H, W), BF16), jax.ShapeDtypeStruct((B, H, W), BF16)),
        in_specs=[three, one],
        out_specs=(three, one),
        scratch_shapes=[pltpu.VMEM((W, W), BF16)],
        compiler_params=pltpu.CompilerParams(vmem_limit_bytes=60 * 1024 * 1024),
    )(along, averaged)
    return velocity[None], template


def solution(mesh):
    return jax.shard_map(
        shards,
        mesh=mesh,
        in_specs=(
            P("subj", "depth", None, None),
            P("subj", "depth"),
            P("subj", "depth", None),
            P("subj", "depth", None),
        ),
        out_specs=(P("subj", None, "depth", None, None), P("depth", None, None)),
        check_vma=False,
    )
```

```python
import math

import jax
import jax.numpy as jnp
from jax import lax
from jax.experimental import pallas as pl
from jax.experimental.pallas import tpu as pltpu
from jax.sharding import PartitionSpec as P

MESH = pl.DeviceIdType.MESH
F32, BF16 = jnp.float32, jnp.bfloat16
H = W = 256
B = 8
HALO = 6
NE = B + 2 * HALO
PAD = 16
EPS = 1e-5
SRC = (0, 48, 96, 144, 176, 208, 240, 256)
C = len(SRC) - 1


def lagging(ends):
    return tuple(max(e - 16, 0) if e < H else H for e in ends)


WE = lagging(SRC)
FE = lagging(WE)
NF = max(FE[i + 1] - FE[i] for i in range(C))
G = 16
U = 4
Z = 4

SRC_R, SRC_L, W_R, W_L, W_C, S_Z, T_C, T_R, T_L, R_L, R_R = range(11)


def taps():
    raw = [math.exp(-(t * t) / 4.5) for t in range(-4, 5)]
    total = sum(raw)
    return [r / total for r in raw]


def iota(shape, dim):
    return lax.broadcasted_iota(jnp.int32, shape, dim)


def gauss_matrix(rows, cols, shift):
    away = jnp.abs(iota((rows, cols), 0) + shift - iota((rows, cols), 1))
    w = taps()
    out = jnp.zeros((rows, cols), F32)
    for t in range(5):
        out = jnp.where(away == t, F32(w[4 + t]), out)
    return out.astype(BF16)


def dot(a, b):
    return jnp.dot(a, b, preferred_element_type=F32)


def rounded_gain():
    import numpy as np
    import ml_dtypes
    w = np.array(taps(), np.float32)
    return float(w.sum()) / float(w.astype(ml_dtypes.bfloat16).astype(np.float32).sum())


def kernel(vol, dsh, psh, fst, zs_out, tmpl, *refs):
    ext = refs[:C]
    (iext, text, wp, sb, sz, yb, gy, sp, bq, gxs, fo, zs, ax2, bx3, dx, ssem, rsem, lsem) = refs[C:]
    me, d = lax.axis_index("subj"), lax.axis_index("depth")
    nd = lax.axis_size("depth")
    core = lax.rem(me, 2)
    mate = me + 1 - 2 * core
    far = lax.rem(me + 2, 4)
    right, left = lax.rem(d + 1, nd), lax.rem(d + nd - 1, nd)
    has_l, has_r = d > 0, d < nd - 1

    def remote(src, dst, p, kind, subj, depth):
        return pltpu.make_async_remote_copy(
            src_ref=src, dst_ref=dst, send_sem=ssem.at[p, kind], recv_sem=rsem.at[p, kind],
            device_id={"subj": subj, "depth": depth}, device_id_type=MESH)

    barrier = pltpu.get_barrier_semaphore()

    def greet(subj, depth):
        pl.semaphore_signal(barrier, inc=1, device_id={"subj": subj, "depth": depth}, device_id_type=MESH)

    greet(mate, d)
    greet(far, d)

    @pl.when(has_l)
    def _():
        greet(me, left)

    @pl.when(has_r)
    def _():
        greet(me, right)

    mine = pl.ds(pl.multiple_of(core * 128, 128), 128)
    other = pl.ds(pl.multiple_of((1 - core) * 128, 128), 128)

    def rows_of(ends, p):
        return pl.ds(ends[p], ends[p + 1] - ends[p])

    def padded_rows(ends, p):
        return pl.ds(PAD + ends[p], ends[p + 1] - ends[p])

    def copy_of(p, kind):
        if kind == SRC_R:
            return remote(vol.at[:, rows_of(SRC, p), :], ext[p].at[0:B], p, kind, me, right)
        if kind == SRC_L:
            return remote(vol.at[:, rows_of(SRC, p), :], ext[p].at[2 * B:3 * B], p, kind, me, left)
        r, q = rows_of(WE, p), padded_rows(WE, p)
        if kind == W_R:
            return remote(iext.at[B:B + HALO, q, :], iext.at[0:HALO, q, :], p, kind, me, right)
        if kind == W_L:
            return remote(iext.at[HALO:2 * HALO, q, :], iext.at[B + HALO:NE, q, :], p, kind, me, left)
        if kind == W_C:
            return remote(iext.at[HALO:HALO + B, q, other], wp.at[:, r, :], p, kind, mate, d)
        if kind == S_Z:
            return remote(sb.at[:, r, :], sz.at[:, r, :], p, kind, far, d)
        if kind == T_C:
            part = text.at[HALO:HALO + B, q, mine]
            return remote(part, part, p, kind, mate, d)
        if kind == T_R:
            return remote(text.at[B:B + HALO, q, mine], text.at[0:HALO, q, mine], p, kind, me, right)
        if kind == T_L:
            return remote(text.at[HALO:2 * HALO, q, mine], text.at[B + HALO:NE, q, mine], p, kind, me, left)
        part = text.at[0:HALO, q, mine] if kind == R_L else text.at[B + HALO:NE, q, mine]
        return remote(part, part, p, kind, mate, d)

    sends = {SRC_R: has_r, W_R: has_r, T_R: has_r, SRC_L: has_l, W_L: has_l, T_L: has_l, R_L: has_l, R_R: has_r}
    gets = {SRC_R: has_l, W_R: has_l, T_R: has_l, SRC_L: has_r, W_L: has_r, T_L: has_r, R_L: has_l, R_R: has_r}

    def start(p, *kinds):
        for kind in kinds:
            if kind in sends:
                pl.when(sends[kind])(lambda kind=kind: copy_of(p, kind).start())
            else:
                copy_of(p, kind).start()

    def landed(p, *kinds):
        for kind in kinds:
            if kind in gets:
                pl.when(gets[kind])(lambda kind=kind: copy_of(p, kind).wait_recv())
            else:
                copy_of(p, kind).wait_recv()

    def own_copy(p):
        return pltpu.make_async_copy(vol.at[:, rows_of(SRC, p), :], ext[p].at[B:2 * B], lsem.at[p])

    for p in range(C):
        own_copy(p).start()

    pl.semaphore_wait(barrier, 2 + has_l.astype(jnp.int32) + has_r.astype(jnp.int32))
    for p in range(C):
        start(p, SRC_R, SRC_L)

    dz, dy, dxs = dsh[0], psh[0], psh[1]
    fz, fy, fx = fst[0].astype(F32) * 0.25, fst[1].astype(F32) * 0.25, fst[2].astype(F32) * 0.25

    def zero_pads(ref, count):
        zero = jnp.zeros((PAD, W), BF16)

        def body(z, carry):
            ref[z, 0:PAD, :] = zero
            ref[z, PAD + H:2 * PAD + H, :] = zero
            return carry
        lax.fori_loop(0, count, body, 0)

    zero_pads(iext, NE)
    zero_pads(text, NE)

    def zero_planes(lo):
        def body(z, carry):
            zero = jnp.zeros((H, W), BF16)
            iext[lo + z, PAD:PAD + H, :] = zero
            text[lo + z, PAD:PAD + H, :] = zero
            return carry
        lax.fori_loop(0, HALO, body, 0)

    @pl.when(d == 0)
    def _():
        zero_planes(0)
        for p in range(C):
            ext[p][0:B] = jnp.zeros((B,) + ext[p].shape[1:], BF16)

    @pl.when(d == nd - 1)
    def _():
        zero_planes(B + HALO)
        for p in range(C):
            ext[p][2 * B:3 * B] = jnp.zeros((B,) + ext[p].shape[1:], BF16)

    row, col = iota((W, W), 0), iota((W, W), 1)
    a_x = jnp.where(row == col + dxs, 1.0 - fx, jnp.where(row == col + dxs + 1, fx, 0.0)).astype(BF16)
    ax2[0:W, :] = a_x
    ax2[W:2 * W, :] = a_x
    b_x = jnp.where(jnp.abs(row - col) <= 2, 1.0, 0.0).astype(BF16)
    for i in range(3):
        bx3[i * W:(i + 1) * W, :] = b_x
    dx[...] = jnp.where(row == col + 1, 0.5, jnp.where(row == col - 1, -0.5, 0.0)).astype(BF16)

    def warp(p):
        a, n = WE[p], WE[p + 1] - WE[p]
        ka = 0 if p == 0 else SRC[p] - 32
        k = SRC[p + 1] - ka
        at, j = iota((n, 2 * k), 0) + (a + dy), iota((n, 2 * k), 1)
        w_z = jnp.where(j < k, 1.0 - fz, fz)
        j = jnp.where(j < k, j, j - k) + ka
        a_y = (w_z * jnp.where(j == at, 1.0 - fy, jnp.where(j == at + 1, fy, 0.0))).astype(BF16)

        for half in range(0, B, U):
            split = []
            for z in range(half, half + U):
                parts = []
                for c in range(2):
                    if p > 0:
                        size = SRC[p] - SRC[p - 1]
                        parts.append(ext[p - 1][8 + dz + z + c, size - 32:size, :])
                    parts.append(ext[p][8 + dz + z + c])
                r = dot(a_y, jnp.concatenate(parts, 0))
                hi = r.astype(BF16)
                lo = (r - hi.astype(F32)).astype(BF16)
                split.append(jnp.concatenate([hi, lo], 1))
            out = dot(jnp.concatenate(split, 0), ax2[...]).astype(BF16)
            iext[HALO + half:HALO + half + U, PAD + a:PAD + a + n, :] = out.reshape(U, n, W)

    def partial_sum(p):
        r, q = rows_of(WE, p), padded_rows(WE, p)

        def body(z, carry):
            sb[z, r, :] = (iext[HALO + z, q, mine].astype(F32) + wp[z, r, :].astype(F32)).astype(BF16)
            return carry
        lax.fori_loop(0, B, body, 0)

    def template(p):
        r, q = rows_of(WE, p), padded_rows(WE, p)

        def body(z, carry):
            text[HALO + z, q, mine] = ((sb[z, r, :].astype(F32) + sz[z, r, :].astype(F32)) * 0.25).astype(BF16)
            return carry
        lax.fori_loop(0, B, body, 0)

    def force(p):
        a, n = FE[p], FE[p + 1] - FE[p]
        k = n + 2 * PAD
        away = iota((n, k), 0) + PAD - iota((n, k), 1)
        b_y = jnp.where(jnp.abs(away) <= 2, 1.0, 0.0).astype(BF16)
        d_y = jnp.where(away == -1, 0.5, jnp.where(away == 1, -0.5, 0.0)).astype(BF16)
        bd = jnp.concatenate([b_y, d_y], 0)
        b2 = jnp.concatenate([b_y, b_y], 1)

        def in_rows(z):
            i, j = iext[z, a:a + k, :], text[z, a:a + k, :]
            both = dot(bd, i)
            yb[0, z, 0:n, :] = both[:n]
            gy[z, 0:n, :] = both[n:]
            yb[1, z, 0:n, :] = dot(b_y, j)
            fi, fj = i.astype(F32), j.astype(F32)
            for q, v in ((2, fi * fj), (3, fi * fi), (4, fj * fj)):
                hi = v.astype(BF16)
                lo = (v - hi.astype(F32)).astype(BF16)
                yb[q, z, 0:n, :] = dot(b2, jnp.concatenate([hi, lo], 0))

        def in_rows_of(zu, carry):
            for u in range(U):
                in_rows(zu * U + u)
            return carry
        lax.fori_loop(0, NE // U, in_rows_of, 0)

        def planes(zu, carry):
            z0 = zu * U
            for q in range(5):
                for g in range(0, n, G):
                    v = [yb[q, z0 + t, g:g + G, :] for t in range(8)]
                    m12, m34, m56 = v[1] + v[2], v[3] + v[4], v[5] + v[6]
                    low, high = m12 + m34, m34 + m56
                    for u, s in enumerate((v[0] + low, low + v[5], v[2] + high, high + v[7])):
                        at = (u * 5 + q) * n + g
                        for part in range(3):
                            piece = s.astype(BF16)
                            sp[at:at + G, part * W:(part + 1) * W] = piece
                            if part < 2:
                                s = s - piece.astype(F32)
            bq[0:5 * U * n, :] = dot(sp[0:5 * U * n, :], bx3[...])
            gxs[0:U * n, :] = dot(iext[pl.ds(z0 + 2, U), PAD + a:PAD + a + n, :].reshape(U * n, W), dx[...])
            for u in range(U):
                z = z0 + u
                whole = (d * B - 4 + z >= 0) & (d * B - 4 + z < nd * B)
                for g in range(0, n, G):
                    here = slice(PAD + a + g, PAD + a + g + G)
                    b_i, b_j, b_ij, b_ii, b_jj = (
                        bq[(u * 5 + q) * n + g:(u * 5 + q) * n + g + G, :] * (1 / 125) for q in range(5))
                    cov = b_ij - b_i * b_j
                    v_i = b_ii - b_i * b_i + EPS
                    v_j = b_jj - b_j * b_j + EPS
                    scaled = cov / (v_i * v_j)
                    i, j = iext[z + 2, here, :].astype(F32), text[z + 2, here, :].astype(F32)
                    common = 2.0 * scaled * ((j - b_j) - scaled * v_j * (i - b_i))
                    common = jnp.where(whole, common, 0.0)
                    g_z = (iext[z + 3, here, :].astype(F32) - iext[z + 1, here, :].astype(F32)) * 0.5
                    fo[0, z, g:g + G, :] = (common * g_z).astype(BF16)
                    fo[1, z, g:g + G, :] = (common * gy[z + 2, g:g + G, :]).astype(BF16)
                    fo[2, z, g:g + G, :] = (common * gxs[u * n + g:u * n + g + G, :]).astype(BF16)
            return carry
        lax.fori_loop(0, 2 * B // U, planes, 0)

        w = [8.0 * rounded_gain() ** 2 * t for t in taps()]

        def along_depth(g, carry):
            r = pl.ds(pl.multiple_of(g * G, G), G)
            out = pl.ds(pl.multiple_of(a + g * G, G), G)
            for k3 in range(3):
                for half in range(2):
                    lanes = slice(half * 128, half * 128 + 128)
                    f = [fo[k3, z, r, lanes].astype(F32) for z in range(2 * B)]
                    for z in range(B):
                        s = f[z + 4] * w[4]
                        for t in range(1, 5):
                            s = s + (f[z + 4 - t] + f[z + 4 + t]) * w[4 + t]
                        zs[k3, z, out, lanes] = s.astype(BF16)
            return carry
        lax.fori_loop(0, n // G, along_depth, 0)

    def out_copy(p):
        r = rows_of(FE, p)
        return pltpu.make_async_copy(zs.at[:, :, r, :], zs_out.at[:, :, r, :], lsem.at[C + p])

    whole_template = pltpu.make_async_copy(
        text.at[HALO:HALO + B, PAD:PAD + H, :], tmpl, lsem.at[2 * C])
    for step, p in (
            ('s', 0),
            ('c', 0),
            ('w', 0),
            ('s', 1),
            ('c', 1),
            ('w', 1),
            ('t', 0),
            ('s', 2),
            ('c', 2),
            ('w', 2),
            ('r', 0),
            ('t', 1),
            ('f', 0),
            ('s', 3),
            ('c', 3),
            ('w', 3),
            ('r', 1),
            ('t', 2),
            ('f', 1),
            ('s', 4),
            ('c', 4),
            ('w', 4),
            ('r', 2),
            ('t', 3),
            ('f', 2),
            ('s', 5),
            ('c', 5),
            ('w', 5),
            ('r', 3),
            ('t', 4),
            ('f', 3),
            ('s', 6),
            ('c', 6),
            ('w', 6),
            ('r', 4),
            ('t', 5),
            ('f', 4),
            ('r', 5),
            ('t', 6),
            ('f', 5),
            ('r', 6),
            ('f', 6)):
        if step == "s":
            own_copy(p).wait()
            landed(p, SRC_R, SRC_L)
            warp(p)
            start(p, W_C)
        elif step == "c":
            landed(p, W_C)
            partial_sum(p)
            start(p, S_Z)
        elif step == "w":
            start(p, W_R, W_L)
        elif step == "t":
            landed(p, S_Z)
            template(p)
            start(p, T_R, T_L, T_C)
        elif step == "r":
            landed(p, T_R, T_L)
            start(p, R_L, R_R)
        elif step == "f":
            landed(p, W_R, W_L, T_C, R_L, R_R)
            if p == C - 1:
                whole_template.start()
            force(p)
            out_copy(p).start()

    for p in range(C):
        out_copy(p).wait()
    whole_template.wait()
    for p in range(C):
        for kind in range(11):
            if kind in sends:
                pl.when(sends[kind])(lambda kind=kind: copy_of(p, kind).wait_send())
            else:
                copy_of(p, kind).wait_send()


def smooth_in_plane(along, averaged, velocity, template, g):
    @pl.when(pl.program_id(0) == 0)
    def _():
        g[...] = gauss_matrix(W, W, 0)

    r = [dot(g[...], along[k3, z]).astype(BF16) for k3 in range(3) for z in range(Z)]
    out = dot(jnp.concatenate(r, 0), g[...]).astype(BF16)
    velocity[...] = out.reshape(3, Z, H, W)
    template[...] = averaged[...]


def shards(volumes, depth_shift, plane_shift, fraction_steps):
    smem = pl.BlockSpec(memory_space=pltpu.SMEM)
    anywhere = pl.BlockSpec(memory_space=pl.ANY)
    scratch = [pltpu.VMEM((3 * B, SRC[p + 1] - SRC[p], W), BF16) for p in range(C)]
    scratch += [
        pltpu.VMEM((NE, H + 2 * PAD, W), BF16),
        pltpu.VMEM((NE, H + 2 * PAD, W), BF16),
        pltpu.VMEM((B, H, 128), BF16),
        pltpu.VMEM((B, H, 128), BF16),
        pltpu.VMEM((B, H, 128), BF16),
        pltpu.VMEM((5, NE, NF, W), F32),
        pltpu.VMEM((NE, NF, W), F32),
        pltpu.VMEM((5 * U * NF, 3 * W), BF16),
        pltpu.VMEM((5 * U * NF, W), F32),
        pltpu.VMEM((U * NF, W), F32),
        pltpu.VMEM((3, 2 * B, NF, W), BF16),
        pltpu.VMEM((3, B, H, W), BF16),
        pltpu.VMEM((2 * W, W), BF16),
        pltpu.VMEM((3 * W, W), BF16),
        pltpu.VMEM((W, W), BF16),
        pltpu.SemaphoreType.DMA((C, 11)),
        pltpu.SemaphoreType.DMA((C, 11)),
        pltpu.SemaphoreType.DMA((2 * C + 1,)),
    ]
    along, averaged = pl.pallas_call(
        kernel,
        out_shape=(jax.ShapeDtypeStruct((3, B, H, W), BF16), jax.ShapeDtypeStruct((B, H, W), BF16)),
        in_specs=[anywhere, smem, smem, smem],
        out_specs=(anywhere, anywhere),
        scratch_shapes=scratch,
        compiler_params=pltpu.CompilerParams(
            collective_id=0, has_side_effects=True, vmem_limit_bytes=56 * 1024 * 1024),
    )(volumes[0], depth_shift.reshape(1), plane_shift.reshape(2), fraction_steps.reshape(3))
    three = pl.BlockSpec((3, Z, H, W), lambda z: (0, z, 0, 0))
    one = pl.BlockSpec((Z, H, W), lambda z: (z, 0, 0))
    velocity, template = pl.pallas_call(
        smooth_in_plane,
        grid=(B // Z,),
        out_shape=(jax.ShapeDtypeStruct((3, B, H, W), BF16), jax.ShapeDtypeStruct((B, H, W), BF16)),
        in_specs=[three, one],
        out_specs=(three, one),
        scratch_shapes=[pltpu.VMEM((W, W), BF16)],
        compiler_params=pltpu.CompilerParams(vmem_limit_bytes=60 * 1024 * 1024),
    )(along, averaged)
    return velocity[None], template


def solution(mesh):
    return jax.shard_map(
        shards,
        mesh=mesh,
        in_specs=(
            P("subj", "depth", None, None),
            P("subj", "depth"),
            P("subj", "depth", None),
            P("subj", "depth", None),
        ),
        out_specs=(P("subj", None, "depth", None, None), P("depth", None, None)),
        check_vma=False,
    )
```
